1024 devices in a mesh: tensor: 8 (over y_hi, core), context: 64 (over z, x), dp: 2 (over y_lo).
Axes of the slice: x: 8, y: 8 (y_hi: 4, y_lo: 2; y = y_hi * 2 + y_lo), z: 8, core: 2. Of those that a mesh axis runs over, the one named last changes fastest.
Arguments:
- queries: bfloat16 [2, 8192, 4096], P('dp', 'context', 'tensor'), may hold values from -6 to 6
- key_gates: bfloat16 [2, 8192, 4096], P('dp', 'context', 'tensor'), may hold values from -6 to 6
- values: bfloat16 [2, 8192, 4096], P('dp', 'context', 'tensor'), may hold values from -6 to 6
- out_grad: bfloat16 [2, 8192, 4096], P('dp', 'context', 'tensor'), may hold values from -6 to 6
- featurizer: bfloat16 [3, 3, 4096], P(None, None, 'tensor'), may hold values from -3.5 to 3.5
- long_filter: bfloat16 [8192, 4096], P('context', 'tensor'), may hold values from -2 to 2
Outputs:
- output: bfloat16 [2, 8192, 4096], P('dp', 'context', 'tensor')
- grad_queries: bfloat16 [2, 8192, 4096], P('dp', 'context', 'tensor')
- grad_keys: bfloat16 [2, 8192, 4096], P('dp', 'context', 'tensor')
- grad_values: bfloat16 [2, 8192, 4096], P('dp', 'context', 'tensor')
- grad_long: bfloat16 [8192, 4096], P('context', 'tensor')
The draws below stay inside these ranges and needn't reach their ends.
All inputs are finite; a program needn't handle non-finite values.
Results may differ from the reference program's by a relative error of at most 0.015.
Values may be sent and summed in bfloat16 or wider, within the bound.
A program may use at most 32 MiB of HBM per device.

```python
import jax
import jax.numpy as jnp
from jax import lax

D = 4096
KTAPS = 3
SEQ_LEN = 8192
SEQS = 2


def draw_long_filter(key, part):
    subkeys = jax.random.split(key, 10)
    delay_offsets = jnp.arange(SEQ_LEN, dtype=jnp.float32)[:, None]
    chooser = jax.random.uniform(subkeys[0], (1, D))
    fast_len = jax.random.uniform(subkeys[1], (1, D), minval=30.0, maxval=50.0)
    slow_len = SEQ_LEN * jax.random.uniform(subkeys[2], (1, D), minval=1.0, maxval=8.0)
    fast_share = 0.5
    is_fast = chooser < fast_share
    decay_len = jnp.where(is_fast, fast_len, slow_len)
    decay_window = jnp.exp(-delay_offsets / decay_len)
    token_places = jax.random.randint(subkeys[3], (3, D), 1, SEQ_LEN)
    dropped_entries = jax.random.uniform(subkeys[4], (3, D), minval=0.5, maxval=0.8)
    for impulse_spike in range(3):
        decay_window = decay_window * jnp.where(delay_offsets >= token_places[impulse_spike][None, :].astype(jnp.float32), dropped_entries[impulse_spike][None, :], 1.0)
    amplitude = 1.5 / jnp.sqrt(jnp.minimum(decay_len, float(SEQ_LEN)))
    noise = jnp.clip(jax.random.normal(subkeys[5], (SEQ_LEN, D)), -4.0, 4.0)
    value = noise * decay_window * amplitude
    echo_start = jax.random.randint(subkeys[7], (1, D), SEQ_LEN // 8, SEQ_LEN // 2).astype(jnp.float32)
    echo_len = float(SEQ_LEN) * jax.random.uniform(subkeys[8], (1, D), minval=0.5, maxval=2.0)
    echo_noise = jnp.clip(jax.random.normal(subkeys[9], (SEQ_LEN, D)), -4.0, 4.0)
    echo_window = jnp.where(delay_offsets >= echo_start, jnp.exp(-jnp.maximum(delay_offsets - echo_start, 0.0) / echo_len), 0.0)
    echo_term = echo_noise * echo_window * (2.0 / jnp.sqrt(float(SEQ_LEN)))
    value = value + jnp.where(is_fast, echo_term, 0.0)
    direct = jax.random.uniform(subkeys[6], (1, D), minval=-2.0, maxval=2.0)
    value = jnp.where(delay_offsets == 0.0, direct, value)
    return jnp.clip(value, -2.0, 2.0).astype(jnp.bfloat16)


def block_levels(own_key, dims, cuts, low, largest):
    level = 1.0
    for axis_at, shards_of in cuts:
        heights = jax.random.uniform(jax.random.fold_in(jax.random.fold_in(own_key, 6), axis_at), (shards_of,), jnp.float32, low / len(cuts), largest / len(cuts))
        level = level * jnp.repeat(jnp.exp(heights), dims[axis_at] // shards_of).reshape((-1,) + (1,) * (len(dims) - 1 - axis_at))
    return level


def centred(own_key, extent, spread, limit, pieces=(), kind=jnp.bfloat16):
    drawn = jax.random.normal(own_key, extent, jnp.float32) * spread
    if len(pieces) > 0:
        drawn = block_levels(own_key, extent, pieces, -0.22, 0.18) * drawn
    return jnp.clip(drawn, min=-limit, max=limit).astype(kind)


def setup_inputs(seed: int = 0) -> dict:
    splits = jax.random.split(jax.random.key(seed), 7)
    return {
        "queries": centred(splits[0], (SEQS, SEQ_LEN, D), 1.0, 6.0, ((0, 2), (1, 64), (2, 8))),
        "key_gates": centred(splits[1], (SEQS, SEQ_LEN, D), 1.0, 6.0, ((0, 2), (1, 64), (2, 8))),
        "values": centred(splits[2], (SEQS, SEQ_LEN, D), 1.0, 6.0, ((0, 2), (1, 64), (2, 8))),
        "out_grad": centred(splits[3], (SEQS, SEQ_LEN, D), 1.0, 6.0, ((0, 2), (1, 64), (2, 8))),
        "featurizer": centred(splits[4], (3, KTAPS, D), KTAPS ** -0.5, 3.5, ((2, 8),)),
        "long_filter": draw_long_filter(jax.random.fold_in(splits[6], 71), 0),
    }


def apply_taps(extended, tap_rows, along_axis, length, forward):
    tap_count = tap_rows.shape[0]
    tap_total = None
    for lag in range(tap_count):
        slice_start = tap_count - 1 - lag if forward else lag
        tap_piece = lax.slice_in_dim(extended, slice_start, slice_start + length, axis=along_axis)
        tap_term = tap_rows[lag] * tap_piece
        tap_total = tap_term if tap_total is None else tap_total + tap_term
    return tap_total


def causal_feat(signal, tap_rows):
    padded = jnp.pad(signal, ((0, 0), (tap_rows.shape[0] - 1, 0), (0, 0)))
    return apply_taps(padded, tap_rows, 1, signal.shape[1], True)


def anticausal_feat(signal, tap_rows):
    padded = jnp.pad(signal, ((0, 0), (0, tap_rows.shape[0] - 1), (0, 0)))
    return apply_taps(padded, tap_rows, 1, signal.shape[1], False)


def reference(queries, key_gates, values, out_grad, featurizer, long_filter):
    block_width = 256
    block_count = D // block_width
    length = SEQ_LEN
    spectrum_len = 2 * length

    def one_block(block_index):
        offset = block_index * block_width

        def slice_block(array):
            return lax.dynamic_slice_in_dim(array, offset, block_width, array.ndim - 1)

        query_block = slice_block(queries).astype(jnp.float32)
        key_block = slice_block(key_gates).astype(jnp.float32)
        value_block = slice_block(values).astype(jnp.float32)
        grad_block = slice_block(out_grad).astype(jnp.float32)
        feat_block = slice_block(featurizer).astype(jnp.float32)
        query_feat = causal_feat(query_block, feat_block[0]).astype(jnp.bfloat16).astype(jnp.float32)
        key_feat = causal_feat(key_block, feat_block[1]).astype(jnp.bfloat16).astype(jnp.float32)
        value_features = causal_feat(value_block, feat_block[2]).astype(jnp.bfloat16).astype(jnp.float32)
        gated = (key_feat * value_features).astype(jnp.bfloat16)
        signal_grad = (grad_block * query_feat).astype(jnp.bfloat16)
        gated_spec = jnp.fft.rfft(gated.astype(jnp.float32), n=spectrum_len, axis=1)
        filter_spec = jnp.fft.rfft(slice_block(long_filter).astype(jnp.float32), n=spectrum_len, axis=0)[None]
        grad_spec = jnp.fft.rfft(signal_grad.astype(jnp.float32), n=spectrum_len, axis=1)
        conv_out = jnp.fft.irfft(gated_spec * filter_spec, n=spectrum_len, axis=1)[:, :length].astype(jnp.bfloat16)
        back_out = jnp.fft.irfft(grad_spec * jnp.conj(filter_spec), n=spectrum_len, axis=1)[:, :length].astype(jnp.bfloat16)
        filter_terms = jnp.fft.irfft(grad_spec * jnp.conj(gated_spec), n=spectrum_len, axis=1)[:, :length]
        filter_grad = jnp.sum(filter_terms, axis=0).astype(jnp.bfloat16)
        conv_wide = conv_out.astype(jnp.float32)
        back_wide = back_out.astype(jnp.float32)
        output = (query_feat * conv_wide).astype(jnp.bfloat16)
        query_feat_grad = (grad_block * conv_wide).astype(jnp.bfloat16).astype(jnp.float32)
        key_feat_grad = (back_wide * value_features).astype(jnp.bfloat16).astype(jnp.float32)
        value_feat_grad = (back_wide * key_feat).astype(jnp.bfloat16).astype(jnp.float32)
        grad_queries = anticausal_feat(query_feat_grad, feat_block[0]).astype(jnp.bfloat16)
        grad_keys = anticausal_feat(key_feat_grad, feat_block[1]).astype(jnp.bfloat16)
        grad_values = anticausal_feat(value_feat_grad, feat_block[2]).astype(jnp.bfloat16)
        return output, grad_queries, grad_keys, grad_values, filter_grad

    blocks = lax.map(one_block, jnp.arange(block_count, dtype=jnp.int32))

    def assemble(stacked):
        return jnp.moveaxis(stacked, 0, 2).reshape(stacked.shape[1], stacked.shape[2], block_count * block_width)

    grad_long = jnp.moveaxis(blocks[4], 0, 1).reshape(length, block_count * block_width)
    return assemble(blocks[0]), assemble(blocks[1]), assemble(blocks[2]), assemble(blocks[3]), grad_long
```

```python
import functools
import math

import ml_dtypes
import numpy as np

import jax
import jax.numpy as jnp
from jax import lax
from jax.experimental import pallas as pl
from jax.experimental.pallas import tpu as pltpu
from jax.sharding import PartitionSpec as P

MESH = pl.DeviceIdType.MESH
F32 = jnp.float32
BF16 = jnp.bfloat16


def tables(blocks, width):
    full = 2 * blocks * width
    a = np.arange(blocks) + 0.5
    q = np.arange(blocks)
    p = np.arange(width)
    angle_qa = 2.0 * math.pi * np.outer(a, q) / (2 * blocks)
    first = np.concatenate([np.cos(angle_qa), -np.sin(angle_qa)], axis=0)
    last = np.concatenate([np.cos(angle_qa.T), -np.sin(angle_qa.T)], axis=1) * (2.0 / full)
    angle_ap = 2.0 * math.pi * np.outer(a, p) / full
    twist = np.stack([np.cos(angle_ap), np.sin(angle_ap)])
    angle_pb = 2.0 * math.pi * (np.outer(p, p) % width) / width
    cos, sin = np.cos(angle_pb), np.sin(angle_pb)
    middle = np.block([[cos, -sin], [sin, cos]])
    half = lambda x: jnp.asarray(x.astype(np.float32).astype(ml_dtypes.bfloat16))
    return (
        half(first),
        half(middle),
        half(middle.T),
        half(last),
        jnp.asarray(twist.astype(np.float32)),
    )


def far_first(step, count):
    up = (step + 1) // 2
    return lax.rem(count // 2 + jnp.where(lax.rem(step, 2) == 1, up, count - step // 2), count)


def main_kernel(
    sizes,
    query_ref,
    key_ref,
    value_ref,
    grad_ref,
    feat_ref,
    filt_ref,
    first_ref,
    middle_ref,
    back_middle_ref,
    last_ref,
    twist_ref,
    conv_out,
    back_out,
    lag_out,
    qf_out,
    kf_out,
    vf_out,
    after_out,
    ext,
    rim_send,
    rim_recv,
    after_send,
    after_recv,
    filt_send,
    filt_recv,
    pair_send,
    pair_recv,
    part_send,
    part_recv,
    conv_send,
    conv_recv,
    lag_send,
    lag_recv,
    wide,
    wide_filt,
    turned,
    filt_spec,
    gate_spec,
    grad_spec,
    product,
    send_sems,
    recv_sems,
):
    ctx, chans, fast = sizes
    tokens, width = query_ref.shape
    me = lax.axis_index("context")
    dp = lax.axis_index("dp")
    slow = ctx // fast
    my_slow, my_fast = me // fast, lax.rem(me, fast)
    following, previous = lax.rem(me + 1, ctx), lax.rem(me + ctx - 1, ctx)
    partner = 1 - dp

    barrier = pltpu.get_barrier_semaphore()

    def peer_of(step):
        s, f = far_first(step // fast, slow), far_first(lax.rem(step, fast), fast)
        return lax.rem(my_slow + s, slow) * fast + lax.rem(my_fast + f, fast)

    @pl.loop(0, ctx - 1)
    def _(step):
        pl.semaphore_signal(
            barrier, inc=1, device_id={"context": peer_of(step)}, device_id_type=MESH
        )

    pl.semaphore_signal(barrier, inc=1, device_id={"dp": partner}, device_id_type=MESH)

    def remote(src, dst, which, device):
        return pltpu.make_async_remote_copy(
            src_ref=src,
            dst_ref=dst,
            send_sem=send_sems.at[which],
            recv_sem=recv_sems.at[which],
            device_id=device,
            device_id_type=MESH,
        )

    def scatter(src, dst, which):
        @pl.loop(0, ctx - 1)
        def _(step):
            peer = peer_of(step)
            remote(src.at[peer], dst.at[me], which, {"context": peer}).start()

        dst[me] = src[me]

    def wait_scatter(ref, sems, which):
        rows = ref.at[pl.ds(0, ctx - 1)]
        pltpu.make_async_copy(rows, rows, sems.at[which]).wait()

    filt_send[...] = filt_ref[...].astype(F32).T.reshape(ctx, chans, tokens).astype(BF16)
    tail = pl.ds(tokens - 8, 8)
    rim_send[0, 0:2] = query_ref[tokens - 16 :].astype(F32)[14:]
    rim_send[0, 2:4] = key_ref[tokens - 16 :].astype(F32)[14:]
    rim_send[0, 4:6] = value_ref[tokens - 16 :].astype(F32)[14:]
    rim_send[0, 6:8] = jnp.zeros((2, width), F32)

    pl.semaphore_wait(barrier, ctx)

    rim_copy = remote(rim_send, rim_recv, 0, {"context": following})
    rim_copy.start()
    scatter(filt_send, filt_recv, 1)
    rim_copy.wait()

    keep = jnp.where(me == 0, 0.0, 1.0).astype(F32)

    def featured(rows_ref, which):
        ext[8 : 8 + tokens] = rows_ref[...].astype(F32)
        ext[6:8] = rim_recv[0, 2 * which : 2 * which + 2] * keep
        total = None
        for lag in range(3):
            tap = feat_ref[which, lag : lag + 1, :]
            term = tap * ext[8 - lag : 8 - lag + tokens]
            total = term if total is None else total + term
        return total.astype(BF16)

    query_feat = featured(query_ref, 0)
    qf_out[...] = query_feat
    key_feat = featured(key_ref, 1)
    kf_out[...] = key_feat
    value_feat = featured(value_ref, 2)
    vf_out[...] = value_feat
    gated = (key_feat.astype(F32) * value_feat.astype(F32)).T.reshape(ctx, chans, tokens)
    signal = (grad_ref[...].astype(F32) * query_feat.astype(F32)).T.reshape(ctx, chans, tokens)
    pair_send[...] = jnp.concatenate([gated, signal], axis=1).astype(BF16)
    scatter(pair_send, pair_recv, 2)

    def spectra(wide_ref, rows, start, dest):
        for channel in range(chans):
            grid = wide_ref[pl.ds(start + channel, ctx, stride=rows), :].astype(BF16)
            section = jnp.dot(first_ref[...], grid, preferred_element_type=F32)
            real, imag = section[:ctx], section[ctx:]
            cos, sin = twist_ref[0], twist_ref[1]
            here = pl.ds(channel * ctx, ctx)
            turned[here, 0:tokens] = (real * cos + imag * sin).astype(BF16)
            turned[here, tokens : 2 * tokens] = (imag * cos - real * sin).astype(BF16)
        dest[...] = jnp.dot(turned[...], middle_ref[...], preferred_element_type=F32)

    wait_scatter(filt_recv, recv_sems, 1)
    wide_filt[...] = filt_recv[...].astype(F32).reshape(ctx * chans, tokens)
    spectra(wide_filt, chans, 0, filt_spec)
    wait_scatter(pair_recv, recv_sems, 2)
    wide[...] = pair_recv[...].astype(F32).reshape(ctx * 2 * chans, tokens)
    spectra(wide, 2 * chans, 0, gate_spec)
    spectra(wide, 2 * chans, chans, grad_spec)

    def parts(ref):
        return ref[:, 0:tokens], ref[:, tokens : 2 * tokens]

    def inverse(real, imag, wide_ref, rows, start):
        product[:, 0:tokens] = real.astype(BF16)
        product[:, tokens : 2 * tokens] = imag.astype(BF16)
        gate = jnp.dot(product[...], back_middle_ref[...], preferred_element_type=F32)
        cos, sin = twist_ref[0], twist_ref[1]
        for channel in range(chans):
            piece = gate[channel * ctx : (channel + 1) * ctx]
            real, imag = piece[:, :tokens], piece[:, tokens:]
            stacked = jnp.concatenate([real * cos - imag * sin, imag * cos + real * sin], axis=0)
            wide_ref[pl.ds(start + channel, ctx, stride=rows), :] = jnp.dot(
                last_ref[...], stacked.astype(BF16), preferred_element_type=F32
            )

    gate_real, gate_imag = parts(gate_spec)
    grad_real, grad_imag = parts(grad_spec)
    inverse(
        grad_real * gate_real + grad_imag * gate_imag,
        grad_imag * gate_real - grad_real * gate_imag,
        wide_filt,
        chans,
        0,
    )
    part_send[...] = wide_filt[...].reshape(ctx, chans, tokens).astype(BF16)
    part_copy = remote(part_send, part_recv, 3, {"dp": partner})
    part_copy.start()
    filt_real, filt_imag = parts(filt_spec)
    gate_real, gate_imag = parts(gate_spec)
    inverse(
        gate_real * filt_real - gate_imag * filt_imag,
        gate_real * filt_imag + gate_imag * filt_real,
        wide,
        2 * chans,
        0,
    )
    filt_real, filt_imag = parts(filt_spec)
    grad_real, grad_imag = parts(grad_spec)
    inverse(
        grad_real * filt_real + grad_imag * filt_imag,
        grad_imag * filt_real - grad_real * filt_imag,
        wide,
        2 * chans,
        chans,
    )
    conv_send[...] = wide[...].reshape(ctx, 2 * chans, tokens).astype(BF16)
    scatter(conv_send, conv_recv, 4)
    part_copy.wait()
    lag_send[...] = (part_send[...].astype(F32) + part_recv[...].astype(F32)).astype(BF16)
    scatter(lag_send, lag_recv, 5)

    wait_scatter(conv_recv, recv_sems, 4)
    both = conv_recv[...].astype(F32)
    conv = both[:, :chans].reshape(width, tokens).T
    back = both[:, chans:].reshape(width, tokens).T
    conv_out[...] = conv.astype(BF16)
    back_out[...] = back.astype(BF16)

    def rounded(x):
        return x.astype(BF16).astype(F32)

    head = 16
    after_send[0, 0:2] = rounded(grad_ref[:head].astype(F32) * conv[:head])[:2]
    after_send[0, 2:4] = rounded(vf_out[:head].astype(F32) * back[:head])[:2]
    after_send[0, 4:6] = rounded(kf_out[:head].astype(F32) * back[:head])[:2]
    after_send[0, 6:8] = jnp.zeros((2, width), F32)
    after_copy = remote(after_send, after_recv, 6, {"context": previous})
    after_copy.start()
    wait_scatter(lag_recv, recv_sems, 5)
    lag_out[...] = lag_recv[...].astype(F32).reshape(width, tokens).T.astype(BF16)
    after_copy.wait()
    after_out[...] = after_recv[0] * jnp.where(me == ctx - 1, 0.0, 1.0).astype(F32)
    wait_scatter(filt_send, send_sems, 1)
    wait_scatter(pair_send, send_sems, 2)
    wait_scatter(conv_send, send_sems, 4)
    wait_scatter(lag_send, send_sems, 5)


def final_kernel(
    conv_ref,
    back_ref,
    lag_ref,
    grad_ref,
    qf_ref,
    kf_ref,
    vf_ref,
    after_ref,
    feat_ref,
    out_ref,
    gq_ref,
    gk_ref,
    gv_ref,
    lag_out,
    ext,
):
    tokens = conv_ref.shape[0]
    conv = conv_ref[...].astype(F32)
    back = back_ref[...].astype(F32)
    out_ref[0] = (qf_ref[...].astype(F32) * conv).astype(BF16)

    def unfeatured(rows, which, dest):
        ext[0:tokens] = rows.astype(BF16).astype(F32)
        ext[tokens : tokens + 2] = after_ref[2 * which : 2 * which + 2]
        total = None
        for lag in range(3):
            term = feat_ref[which, lag : lag + 1, :] * ext[lag : lag + tokens]
            total = term if total is None else total + term
        dest[0] = total.astype(BF16)

    unfeatured(grad_ref[...].astype(F32) * conv, 0, gq_ref)
    unfeatured(back * vf_ref[...].astype(F32), 1, gk_ref)
    unfeatured(back * kf_ref[...].astype(F32), 2, gv_ref)
    lag_out[...] = lag_ref[...]


def on_device(ctx, queries, key_gates, values, out_grad, featurizer, long_filter):
    tokens, width = long_filter.shape
    chans = width // ctx
    fast = 8
    consts = tables(ctx, tokens)
    taps = featurizer.astype(F32)
    vmem = pl.BlockSpec(memory_space=pltpu.VMEM)
    like = lambda *shape, dtype=BF16: jax.ShapeDtypeStruct(shape, dtype)
    buf = lambda *shape, dtype=BF16: pltpu.VMEM(shape, dtype)
    results = pl.pallas_call(
        functools.partial(main_kernel, (ctx, chans, fast)),
        out_shape=(
            like(tokens, width),
            like(tokens, width),
            like(tokens, width),
            like(tokens, width),
            like(tokens, width),
            like(tokens, width),
            like(8, width, dtype=F32),
        ),
        in_specs=[vmem] * 11,
        out_specs=(vmem,) * 7,
        scratch_shapes=[
            buf(tokens + 16, width, dtype=F32),
            buf(1, 8, width, dtype=F32),
            buf(1, 8, width, dtype=F32),
            buf(1, 8, width, dtype=F32),
            buf(1, 8, width, dtype=F32),
            buf(ctx, chans, tokens),
            buf(ctx, chans, tokens),
            buf(ctx, 2 * chans, tokens),
            buf(ctx, 2 * chans, tokens),
            buf(ctx, chans, tokens),
            buf(ctx, chans, tokens),
            buf(ctx, 2 * chans, tokens),
            buf(ctx, 2 * chans, tokens),
            buf(ctx, chans, tokens),
            buf(ctx, chans, tokens),
            buf(ctx * 2 * chans, tokens, dtype=F32),
            buf(ctx * chans, tokens, dtype=F32),
            buf(ctx * chans, 2 * tokens),
            buf(ctx * chans, 2 * tokens, dtype=F32),
            buf(ctx * chans, 2 * tokens, dtype=F32),
            buf(ctx * chans, 2 * tokens, dtype=F32),
            buf(ctx * chans, 2 * tokens),
            pltpu.SemaphoreType.DMA((7,)),
            pltpu.SemaphoreType.DMA((7,)),
        ],
        compiler_params=pltpu.CompilerParams(
            collective_id=0, has_side_effects=True, vmem_limit_bytes=48 * 1024 * 1024
        ),
        name="exchange",
    )(queries[0], key_gates[0], values[0], out_grad[0], taps, long_filter, *consts)
    conv, back, lag, qf, kf, vf, after = results
    return pl.pallas_call(
        final_kernel,
        out_shape=(like(1, tokens, width),) * 4 + (like(tokens, width),),
        in_specs=[vmem] * 9,
        out_specs=(vmem,) * 5,
        scratch_shapes=[buf(tokens + 16, width, dtype=F32)],
        compiler_params=pltpu.CompilerParams(vmem_limit_bytes=32 * 1024 * 1024),
        name="finish",
    )(conv, back, lag, out_grad[0], qf, kf, vf, after, taps)


def solution(mesh):
    in_specs = (
        P("dp", "context", "tensor"),
        P("dp", "context", "tensor"),
        P("dp", "context", "tensor"),
        P("dp", "context", "tensor"),
        P(None, None, "tensor"),
        P("context", "tensor"),
    )
    out_specs = (
        P("dp", "context", "tensor"),
        P("dp", "context", "tensor"),
        P("dp", "context", "tensor"),
        P("dp", "context", "tensor"),
        P("context", "tensor"),
    )
    return jax.shard_map(
        functools.partial(on_device, mesh.shape["context"]),
        mesh=mesh,
        in_specs=in_specs,
        out_specs=out_specs,
        check_vma=False,
    )
```

```python
import functools
import math

import ml_dtypes
import numpy as np

import jax
import jax.numpy as jnp
from jax import lax
from jax.experimental import pallas as pl
from jax.experimental.pallas import tpu as pltpu
from jax.sharding import PartitionSpec as P

MESH = pl.DeviceIdType.MESH
F32 = jnp.float32
BF16 = jnp.bfloat16
GRANT = 54240 * 1024


def tables(blocks, width):
    full = 2 * blocks * width
    a = np.arange(blocks) + 0.5
    q = np.arange(blocks)
    p = np.arange(width)
    angle_qa = 2.0 * math.pi * np.outer(a, q) / (2 * blocks)
    first = np.concatenate([np.cos(angle_qa), -np.sin(angle_qa)], axis=0)
    last = np.concatenate([np.cos(angle_qa.T), -np.sin(angle_qa.T)], axis=1) * (2.0 / full)
    angle_ap = 2.0 * math.pi * np.outer(a, p) / full
    twist = np.stack([np.cos(angle_ap), np.sin(angle_ap)])
    angle_pb = 2.0 * math.pi * (np.outer(p, p) % width) / width
    cos, sin = np.cos(angle_pb), np.sin(angle_pb)
    middle = np.block([[cos, -sin], [sin, cos]])
    half = np.zeros((2 * 2 * width + 2 * blocks + blocks, 2 * width), np.float32)
    half[: 2 * width] = middle
    half[2 * width : 4 * width] = middle.T
    half[4 * width : 4 * width + 2 * blocks, :blocks] = first
    half[4 * width + 2 * blocks :, : 2 * blocks] = last
    wide = np.zeros((8 * blocks, width), np.float32)
    wide[: 2 * blocks] = twist.reshape(2 * blocks, width)
    return jnp.asarray(half.astype(ml_dtypes.bfloat16)), jnp.asarray(wide)


def far_first(step, count):
    up = (step + 1) // 2
    return lax.rem(count // 2 + jnp.where(lax.rem(step, 2) == 1, up, count - step // 2), count)


def main_kernel(
    sizes,
    filt_hbm,
    query_hbm,
    key_hbm,
    value_hbm,
    grad_hbm,
    feat_hbm,
    table_hbm,
    twist_hbm,
    conv_out,
    back_out,
    lag_out,
    qf_out,
    kf_out,
    vf_out,
    grad_out,
    after_out,
    taps,
    filt_ref,
    query_ref,
    key_ref,
    value_ref,
    grad_ref,
    feat_ref,
    table_ref,
    twist_ref,
    ext,
    rim_send,
    rim_recv,
    after_send,
    after_recv,
    filt_send,
    filt_recv,
    pair_send,
    pair_recv,
    part_send,
    part_recv,
    conv_send,
    conv_recv,
    lag_send,
    lag_recv,
    wide,
    wide_filt,
    turned,
    filt_spec,
    gate_spec,
    grad_spec,
    product,
    load_sems,
    send_sems,
    recv_sems,
    ring_sem,
):
    ctx, chans, fast = sizes
    tokens, width = query_ref.shape
    middle_rows, back_rows = pl.ds(0, 2 * tokens), pl.ds(2 * tokens, 2 * tokens)
    first_rows, last_rows = pl.ds(4 * tokens, 2 * ctx), pl.ds(4 * tokens + 2 * ctx, ctx)
    me = lax.axis_index("context")
    dp = lax.axis_index("dp")
    slow = ctx // fast
    my_slow, my_fast = me // fast, lax.rem(me, fast)
    following, previous = lax.rem(me + 1, ctx), lax.rem(me + ctx - 1, ctx)
    partner = 1 - dp

    barrier = pltpu.get_barrier_semaphore()

    def peer_of(step):
        s, f = far_first(step // fast, slow), far_first(lax.rem(step, fast), fast)
        return lax.rem(my_slow + s, slow) * fast + lax.rem(my_fast + f, fast)

    def tell(sem, device):
        pl.semaphore_signal(sem, inc=1, device_id=device, device_id_type=MESH)

    def in_slow_ring(step):
        return lax.rem(my_slow + far_first(step, slow), slow) * fast + my_fast

    def in_fast_ring(step):
        return my_slow * fast + lax.rem(my_fast + far_first(step, fast), fast)

    @pl.loop(0, slow - 1)
    def _(step):
        tell(barrier, {"context": in_slow_ring(step)})

    @pl.loop(0, fast - 1)
    def _(step):
        tell(barrier, {"context": in_fast_ring(step)})

    tell(barrier, {"context": following})
    tell(barrier, {"context": previous})
    tell(barrier, {"dp": partner})

    loads = [
        pltpu.make_async_copy(src, dst, load_sems.at[i])
        for i, (src, dst) in enumerate(
            (
                (query_hbm, query_ref),
                (key_hbm, key_ref),
                (value_hbm, value_ref),
                (feat_hbm, feat_ref),
                (grad_hbm, grad_ref),
                (filt_hbm, filt_ref),
                (table_hbm, table_ref),
                (twist_hbm.at[pl.ds(0, 2 * ctx)], twist_ref),
            )
        )
    ]
    for load in loads:
        load.start()

    def remote(src, dst, which, device):
        return pltpu.make_async_remote_copy(
            src_ref=src,
            dst_ref=dst,
            send_sem=send_sems.at[which],
            recv_sem=recv_sems.at[which],
            device_id=device,
            device_id_type=MESH,
        )

    def scatter(src, dst, which):
        @pl.loop(0, ctx - 1)
        def _(step):
            peer = peer_of(step)
            remote(src.at[peer], dst.at[me], which, {"context": peer}).start()

        dst[me] = src[me]

    def wait_scatter(ref, sems, which):
        rows = ref.at[pl.ds(0, ctx - 1)]
        pltpu.make_async_copy(rows, rows, sems.at[which]).wait()

    for load in loads[:3]:
        load.wait()
    for row, rows_ref in enumerate((query_ref, key_ref, value_ref)):
        rim_send[0, 2 * row : 2 * row + 2] = rows_ref[tokens - 16 :].astype(F32)[14:]
    rim_send[0, 6:8] = jnp.zeros((2, width), F32)

    pl.semaphore_wait(barrier, slow + fast + 1)

    rim_copy = remote(rim_send, rim_recv, 0, {"context": following})
    rim_copy.start()

    @pl.loop(0, slow - 1)
    def _(step):
        tell(ring_sem, {"context": in_slow_ring(step)})

    for load in loads[3:]:
        load.wait()
    taps[...] = feat_ref[...].astype(F32)
    filt_send[...] = filt_ref[...].astype(F32).T.reshape(ctx, chans, tokens).astype(BF16)
    rim_copy.wait()

    keep = jnp.where(me == 0, 0.0, 1.0).astype(F32)

    def featured(rows_ref, which):
        ext[8 : 8 + tokens] = rows_ref[...].astype(F32)
        ext[6:8] = rim_recv[0, 2 * which : 2 * which + 2] * keep
        total = None
        for lag in range(3):
            tap = taps[which, lag : lag + 1, :]
            term = tap * ext[8 - lag : 8 - lag + tokens]
            total = term if total is None else total + term
        return total.astype(BF16)

    query_feat = featured(query_ref, 0)
    qf_out[...] = query_feat
    key_feat = featured(key_ref, 1)
    kf_out[...] = key_feat
    value_feat = featured(value_ref, 2)
    vf_out[...] = value_feat
    grad_out[...] = grad_ref[...]
    gated = (key_feat.astype(F32) * value_feat.astype(F32)).T.reshape(ctx, chans, tokens)
    signal = (grad_ref[...].astype(F32) * query_feat.astype(F32)).T.reshape(ctx, chans, tokens)
    pair_send[...] = jnp.concatenate([gated, signal], axis=1).astype(BF16)
    pl.semaphore_wait(ring_sem, slow - 1)
    scatter(pair_send, pair_recv, 2)
    scatter(filt_send, filt_recv, 1)

    def spectra(wide_ref, rows, start, dest):
        for channel in range(chans):
            grid = wide_ref[pl.ds(start + channel, ctx, stride=rows), :].astype(BF16)
            section = jnp.dot(table_ref[first_rows, 0:ctx], grid, preferred_element_type=F32)
            real, imag = section[:ctx], section[ctx:]
            cos, sin = twist_ref[0:ctx], twist_ref[ctx : 2 * ctx]
            here = pl.ds(channel * ctx, ctx)
            turned[here, 0:tokens] = (real * cos + imag * sin).astype(BF16)
            turned[here, tokens : 2 * tokens] = (imag * cos - real * sin).astype(BF16)
        dest[...] = jnp.dot(turned[...], table_ref[middle_rows], preferred_element_type=F32)

    wait_scatter(pair_recv, recv_sems, 2)
    wide[...] = pair_recv[...].astype(F32).reshape(ctx * 2 * chans, tokens)
    spectra(wide, 2 * chans, 0, gate_spec)
    spectra(wide, 2 * chans, chans, grad_spec)

    def parts(ref):
        return ref[:, 0:tokens], ref[:, tokens : 2 * tokens]

    def inverse(real, imag, wide_ref, rows, start):
        product[:, 0:tokens] = real.astype(BF16)
        product[:, tokens : 2 * tokens] = imag.astype(BF16)
        gate = jnp.dot(product[...], table_ref[back_rows], preferred_element_type=F32)
        cos, sin = twist_ref[0:ctx], twist_ref[ctx : 2 * ctx]
        for channel in range(chans):
            piece = gate[channel * ctx : (channel + 1) * ctx]
            real, imag = piece[:, :tokens], piece[:, tokens:]
            stacked = jnp.concatenate([real * cos - imag * sin, imag * cos + real * sin], axis=0)
            wide_ref[pl.ds(start + channel, ctx, stride=rows), :] = jnp.dot(
                table_ref[last_rows, 0 : 2 * ctx], stacked.astype(BF16), preferred_element_type=F32
            )

    gate_real, gate_imag = parts(gate_spec)
    grad_real, grad_imag = parts(grad_spec)
    inverse(
        grad_real * gate_real + grad_imag * gate_imag,
        grad_imag * gate_real - grad_real * gate_imag,
        wide_filt,
        chans,
        0,
    )
    part_send[...] = wide_filt[...].reshape(ctx, chans, tokens).astype(BF16)
    part_copy = remote(part_send, part_recv, 3, {"dp": partner})
    part_copy.start()
    wait_scatter(filt_recv, recv_sems, 1)
    wide_filt[...] = filt_recv[...].astype(F32).reshape(ctx * chans, tokens)
    spectra(wide_filt, chans, 0, filt_spec)
    filt_real, filt_imag = parts(filt_spec)
    gate_real, gate_imag = parts(gate_spec)
    inverse(
        gate_real * filt_real - gate_imag * filt_imag,
        gate_real * filt_imag + gate_imag * filt_real,
        wide,
        2 * chans,
        0,
    )
    filt_real, filt_imag = parts(filt_spec)
    grad_real, grad_imag = parts(grad_spec)
    inverse(
        grad_real * filt_real + grad_imag * filt_imag,
        grad_imag * filt_real - grad_real * filt_imag,
        wide,
        2 * chans,
        chans,
    )
    conv_send[...] = wide[...].reshape(ctx, 2 * chans, tokens).astype(BF16)
    scatter(conv_send, conv_recv, 4)
    part_copy.wait()
    lag_send[...] = (part_send[...].astype(F32) + part_recv[...].astype(F32)).astype(BF16)
    scatter(lag_send, lag_recv, 5)

    wait_scatter(conv_recv, recv_sems, 4)
    both = conv_recv[...].astype(F32)
    conv = both[:, :chans].reshape(width, tokens).T
    back = both[:, chans:].reshape(width, tokens).T
    conv_out[...] = conv.astype(BF16)
    back_out[...] = back.astype(BF16)

    def rounded(x):
        return x.astype(BF16).astype(F32)

    head = 16
    after_send[0, 0:2] = rounded(grad_ref[:head].astype(F32) * conv[:head])[:2]
    after_send[0, 2:4] = rounded(vf_out[:head].astype(F32) * back[:head])[:2]
    after_send[0, 4:6] = rounded(kf_out[:head].astype(F32) * back[:head])[:2]
    after_send[0, 6:8] = jnp.zeros((2, width), F32)
    after_copy = remote(after_send, after_recv, 6, {"context": previous})
    after_copy.start()
    wait_scatter(lag_recv, recv_sems, 5)
    lag_out[...] = lag_recv[...].astype(F32).reshape(width, tokens).T.astype(BF16)
    after_copy.wait()
    after_out[...] = after_recv[0] * jnp.where(me == ctx - 1, 0.0, 1.0).astype(F32)
    wait_scatter(filt_send, send_sems, 1)
    wait_scatter(pair_send, send_sems, 2)
    wait_scatter(conv_send, send_sems, 4)
    wait_scatter(lag_send, send_sems, 5)


def final_kernel(
    conv_ref,
    back_ref,
    lag_ref,
    grad_ref,
    qf_ref,
    kf_ref,
    vf_ref,
    after_ref,
    taps_ref,
    out_ref,
    gq_ref,
    gk_ref,
    gv_ref,
    lag_out,
    ext,
):
    tokens = conv_ref.shape[0]
    conv = conv_ref[...].astype(F32)
    back = back_ref[...].astype(F32)
    out_ref[0] = (qf_ref[...].astype(F32) * conv).astype(BF16)

    def unfeatured(rows, which, dest):
        ext[0:tokens] = rows.astype(BF16).astype(F32)
        ext[tokens : tokens + 2] = after_ref[2 * which : 2 * which + 2]
        total = None
        for lag in range(3):
            term = taps_ref[which, lag : lag + 1, :] * ext[lag : lag + tokens]
            total = term if total is None else total + term
        dest[0] = total.astype(BF16)

    unfeatured(grad_ref[...].astype(F32) * conv, 0, gq_ref)
    unfeatured(back * vf_ref[...].astype(F32), 1, gk_ref)
    unfeatured(back * kf_ref[...].astype(F32), 2, gv_ref)
    lag_out[...] = lag_ref[...]


def on_device(ctx, queries, key_gates, values, out_grad, featurizer, long_filter):
    tokens, width = long_filter.shape
    chans = width // ctx
    fast = 1 << ((ctx.bit_length() - 1) // 2)
    table, twist = tables(ctx, tokens)
    operands = (
        long_filter,
        queries[0],
        key_gates[0],
        values[0],
        out_grad[0],
        featurizer,
        table,
        twist,
    )
    vmem = pl.BlockSpec(memory_space=pltpu.VMEM)
    like = lambda *shape, dtype=BF16: jax.ShapeDtypeStruct(shape, dtype)
    buf = lambda *shape, dtype=BF16: pltpu.VMEM(shape, dtype)
    results = pl.pallas_call(
        functools.partial(main_kernel, (ctx, chans, fast)),
        out_shape=(
            like(tokens, width),
            like(tokens, width),
            like(tokens, width),
            like(tokens, width),
            like(tokens, width),
            like(tokens, width),
            like(tokens, width),
            like(8, width, dtype=F32),
            like(*featurizer.shape, dtype=F32),
        ),
        in_specs=[pl.BlockSpec(memory_space=pltpu.HBM)] * len(operands),
        out_specs=(vmem,) * 9,
        scratch_shapes=[
            *(buf(*x.shape, dtype=x.dtype) for x in operands[:-1]),
            buf(2 * ctx, tokens, dtype=F32),
            buf(tokens + 16, width, dtype=F32),
            buf(1, 8, width, dtype=F32),
            buf(1, 8, width, dtype=F32),
            buf(1, 8, width, dtype=F32),
            buf(1, 8, width, dtype=F32),
            buf(ctx, chans, tokens),
            buf(ctx, chans, tokens),
            buf(ctx, 2 * chans, tokens),
            buf(ctx, 2 * chans, tokens),
            buf(ctx, chans, tokens),
            buf(ctx, chans, tokens),
            buf(ctx, 2 * chans, tokens),
            buf(ctx, 2 * chans, tokens),
            buf(ctx, chans, tokens),
            buf(ctx, chans, tokens),
            buf(ctx * 2 * chans, tokens, dtype=F32),
            buf(ctx * chans, tokens, dtype=F32),
            buf(ctx * chans, 2 * tokens),
            buf(ctx * chans, 2 * tokens, dtype=F32),
            buf(ctx * chans, 2 * tokens, dtype=F32),
            buf(ctx * chans, 2 * tokens, dtype=F32),
            buf(ctx * chans, 2 * tokens),
            pltpu.SemaphoreType.DMA((len(operands),)),
            pltpu.SemaphoreType.DMA((7,)),
            pltpu.SemaphoreType.DMA((7,)),
            pltpu.SemaphoreType.REGULAR,
        ],
        compiler_params=pltpu.CompilerParams(
            collective_id=0, has_side_effects=True, vmem_limit_bytes=GRANT
        ),
        name="exchange",
    )(*operands)
    conv, back, lag, qf, kf, vf, grad, after, taps = results
    return pl.pallas_call(
        final_kernel,
        out_shape=(like(1, tokens, width),) * 4 + (like(tokens, width),),
        in_specs=[vmem] * 9,
        out_specs=(vmem,) * 5,
        scratch_shapes=[buf(tokens + 16, width, dtype=F32)],
        compiler_params=pltpu.CompilerParams(vmem_limit_bytes=32 * 1024 * 1024),
        name="finish",
    )(conv, back, lag, grad, qf, kf, vf, after, taps)


def solution(mesh):
    in_specs = (
        P("dp", "context", "tensor"),
        P("dp", "context", "tensor"),
        P("dp", "context", "tensor"),
        P("dp", "context", "tensor"),
        P(None, None, "tensor"),
        P("context", "tensor"),
    )
    out_specs = (
        P("dp", "context", "tensor"),
        P("dp", "context", "tensor"),
        P("dp", "context", "tensor"),
        P("dp", "context", "tensor"),
        P("context", "tensor"),
    )
    return jax.shard_map(
        functools.partial(on_device, mesh.shape["context"]),
        mesh=mesh,
        in_specs=in_specs,
        out_specs=out_specs,
        check_vma=False,
    )
```

```python
import functools
import math

import ml_dtypes
import numpy as np

import jax
import jax.numpy as jnp
from jax import lax
from jax.experimental import pallas as pl
from jax.experimental.pallas import tpu as pltpu
from jax.sharding import PartitionSpec as P

MESH = pl.DeviceIdType.MESH
F32 = jnp.float32
BF16 = jnp.bfloat16
GRANT = 54240 * 1024


def tables(blocks, width):
    full = 2 * blocks * width
    a = np.arange(blocks) + 0.5
    q = np.arange(blocks)
    p = np.arange(width)
    angle_qa = 2.0 * math.pi * np.outer(a, q) / (2 * blocks)
    first = np.concatenate([np.cos(angle_qa), -np.sin(angle_qa)], axis=0)
    last = np.concatenate([np.cos(angle_qa.T), -np.sin(angle_qa.T)], axis=1) * (2.0 / full)
    angle_ap = 2.0 * math.pi * np.outer(a, p) / full
    twist = np.stack([np.cos(angle_ap), np.sin(angle_ap)])
    angle_pb = 2.0 * math.pi * (np.outer(p, p) % width) / width
    cos, sin = np.cos(angle_pb), np.sin(angle_pb)
    middle = np.block([[cos, -sin], [sin, cos]])
    half = np.zeros((2 * 2 * width + 2 * blocks + blocks, 2 * width), np.float32)
    half[: 2 * width] = middle
    half[2 * width : 4 * width] = middle.T
    half[4 * width : 4 * width + 2 * blocks, :blocks] = first
    half[4 * width + 2 * blocks :, : 2 * blocks] = last
    wide = np.zeros((8 * blocks, width), np.float32)
    wide[: 2 * blocks] = twist.reshape(2 * blocks, width)
    return jnp.asarray(half.astype(ml_dtypes.bfloat16)), jnp.asarray(wide)


def far_first(step, count):
    up = (step + 1) // 2
    return lax.rem(count // 2 + jnp.where(lax.rem(step, 2) == 1, up, count - step // 2), count)


def main_kernel(
    sizes,
    filt_hbm,
    query_hbm,
    key_hbm,
    value_hbm,
    grad_hbm,
    feat_hbm,
    table_hbm,
    twist_hbm,
    conv_out,
    back_out,
    lag_out,
    qf_out,
    kf_out,
    vf_out,
    grad_out,
    after_out,
    taps,
    filt_ref,
    query_ref,
    key_ref,
    value_ref,
    grad_ref,
    feat_ref,
    table_ref,
    twist_ref,
    ext,
    rim_send,
    rim_recv,
    after_send,
    after_recv,
    filt_send,
    filt_mid,
    filt_recv,
    pair_send,
    pair_recv,
    part_recv,
    conv_send,
    conv_recv,
    lag_send,
    lag_recv,
    wide,
    wide_filt,
    turned,
    filt_spec,
    gate_spec,
    grad_spec,
    product,
    load_sems,
    send_sems,
    recv_sems,
    ring_sem,
):
    ctx, chans, fast = sizes
    tokens, width = query_ref.shape
    middle_rows, back_rows = pl.ds(0, 2 * tokens), pl.ds(2 * tokens, 2 * tokens)
    first_rows, last_rows = pl.ds(4 * tokens, 2 * ctx), pl.ds(4 * tokens + 2 * ctx, ctx)
    me = lax.axis_index("context")
    dp = lax.axis_index("dp")
    slow = ctx // fast
    my_slow, my_fast = me // fast, lax.rem(me, fast)
    following, previous = lax.rem(me + 1, ctx), lax.rem(me + ctx - 1, ctx)
    partner = 1 - dp

    barrier = pltpu.get_barrier_semaphore()

    def peer_of(step):
        s, f = far_first(step // fast, slow), far_first(lax.rem(step, fast), fast)
        return lax.rem(my_slow + s, slow) * fast + lax.rem(my_fast + f, fast)

    def tell(sem, device):
        pl.semaphore_signal(sem, inc=1, device_id=device, device_id_type=MESH)

    def in_slow_ring(step):
        return lax.rem(my_slow + far_first(step, slow), slow) * fast + my_fast

    def in_fast_ring(step):
        return my_slow * fast + lax.rem(my_fast + far_first(step, fast), fast)

    @pl.loop(0, slow - 1)
    def _(step):
        tell(barrier, {"context": in_slow_ring(step)})

    @pl.loop(0, fast - 1)
    def _(step):
        tell(barrier, {"context": in_fast_ring(step)})

    tell(barrier, {"context": following})
    tell(barrier, {"context": previous})
    tell(barrier, {"dp": partner})

    loads = [
        pltpu.make_async_copy(src, dst, load_sems.at[i])
        for i, (src, dst) in enumerate(
            (
                (query_hbm, query_ref),
                (key_hbm, key_ref),
                (value_hbm, value_ref),
                (feat_hbm, feat_ref),
                (grad_hbm, grad_ref),
                (filt_hbm, filt_ref),
                (table_hbm, table_ref),
                (twist_hbm.at[pl.ds(0, 2 * ctx)], twist_ref),
            )
        )
    ]
    for load in loads:
        load.start()

    def remote(src, dst, which, device):
        return pltpu.make_async_remote_copy(
            src_ref=src,
            dst_ref=dst,
            send_sem=send_sems.at[which],
            recv_sem=recv_sems.at[which],
            device_id=device,
            device_id_type=MESH,
        )

    def scatter(src, dst, which):
        @pl.loop(0, ctx - 1)
        def _(step):
            peer = peer_of(step)
            remote(src.at[peer], dst.at[me], which, {"context": peer}).start()

        dst[me] = src[me]

    def ring_scatter(src, dst, place, mine, count, which):
        @pl.loop(0, count - 1)
        def _(step):
            at = lax.rem(mine + far_first(step, count), count)
            remote(src.at[:, at], dst.at[mine], which, {"context": place(step)}).start()

        dst[mine] = src[:, mine]

    def wait_scatter(ref, sems, which):
        rows = ref.at[pl.ds(0, ref.shape[0] - 1)]
        pltpu.make_async_copy(rows, rows, sems.at[which]).wait()

    for load in loads[:3]:
        load.wait()
    for row, rows_ref in enumerate((query_ref, key_ref, value_ref)):
        rim_send[0, 2 * row : 2 * row + 2] = rows_ref[tokens - 16 :].astype(F32)[14:]
    rim_send[0, 6:8] = jnp.zeros((2, width), F32)

    for load in loads[3:]:
        load.wait()
    taps[...] = feat_ref[...].astype(F32)
    by_channel = filt_ref[...].astype(F32).T.reshape(slow, fast, chans, tokens)
    filt_send[...] = by_channel.astype(BF16)

    pl.semaphore_wait(barrier, slow + fast + 1)

    rim_copy = remote(rim_send, rim_recv, 0, {"context": following})
    rim_copy.start()

    @pl.loop(0, slow - 1)
    def _(step):
        tell(ring_sem, {"context": in_slow_ring(step)})

    ring_scatter(filt_send, filt_mid, in_fast_ring, my_fast, fast, 1)
    rim_copy.wait()

    keep = jnp.where(me == 0, 0.0, 1.0).astype(F32)

    def featured(rows_ref, which):
        ext[8 : 8 + tokens] = rows_ref[...].astype(F32)
        ext[6:8] = rim_recv[0, 2 * which : 2 * which + 2] * keep
        total = None
        for lag in range(3):
            tap = taps[which, lag : lag + 1, :]
            term = tap * ext[8 - lag : 8 - lag + tokens]
            total = term if total is None else total + term
        return total.astype(BF16)

    query_feat = featured(query_ref, 0)
    qf_out[...] = query_feat
    key_feat = featured(key_ref, 1)
    kf_out[...] = key_feat
    value_feat = featured(value_ref, 2)
    vf_out[...] = value_feat
    grad_out[...] = grad_ref[...]
    gated = (key_feat.astype(F32) * value_feat.astype(F32)).T.reshape(ctx, chans, tokens)
    signal = (grad_ref[...].astype(F32) * query_feat.astype(F32)).T.reshape(ctx, chans, tokens)
    pair_send[...] = jnp.concatenate([gated, signal], axis=1).astype(BF16)
    pl.semaphore_wait(ring_sem, slow - 1)
    scatter(pair_send, pair_recv, 2)
    wait_scatter(filt_mid, recv_sems, 1)
    ring_scatter(filt_mid, filt_recv, in_slow_ring, my_slow, slow, 7)

    def spectra(wide_ref, rows, start, dest):
        for channel in range(chans):
            grid = wide_ref[pl.ds(start + channel, ctx, stride=rows), :].astype(BF16)
            section = jnp.dot(table_ref[first_rows, 0:ctx], grid, preferred_element_type=F32)
            real, imag = section[:ctx], section[ctx:]
            cos, sin = twist_ref[0:ctx], twist_ref[ctx : 2 * ctx]
            here = pl.ds(channel * ctx, ctx)
            turned[here, 0:tokens] = (real * cos + imag * sin).astype(BF16)
            turned[here, tokens : 2 * tokens] = (imag * cos - real * sin).astype(BF16)
        dest[...] = jnp.dot(turned[...], table_ref[middle_rows], preferred_element_type=F32)

    wait_scatter(pair_recv, recv_sems, 2)
    wide[...] = pair_recv[...].astype(F32).reshape(ctx * 2 * chans, tokens)
    spectra(wide, 2 * chans, 0, gate_spec)
    spectra(wide, 2 * chans, chans, grad_spec)

    def parts(ref):
        return ref[:, 0:tokens], ref[:, tokens : 2 * tokens]

    def inverse(real, imag, wide_ref, rows, start):
        product[:, 0:tokens] = real.astype(BF16)
        product[:, tokens : 2 * tokens] = imag.astype(BF16)
        gate = jnp.dot(product[...], table_ref[back_rows], preferred_element_type=F32)
        cos, sin = twist_ref[0:ctx], twist_ref[ctx : 2 * ctx]
        for channel in range(chans):
            piece = gate[channel * ctx : (channel + 1) * ctx]
            real, imag = piece[:, :tokens], piece[:, tokens:]
            stacked = jnp.concatenate([real * cos - imag * sin, imag * cos + real * sin], axis=0)
            wide_ref[pl.ds(start + channel, ctx, stride=rows), :] = jnp.dot(
                table_ref[last_rows, 0 : 2 * ctx], stacked.astype(BF16), preferred_element_type=F32
            )

    gate_real, gate_imag = parts(gate_spec)
    grad_real, grad_imag = parts(grad_spec)
    inverse(
        grad_real * gate_real + grad_imag * gate_imag,
        grad_imag * gate_real - grad_real * gate_imag,
        wide_filt,
        chans,
        0,
    )
    lag_send[...] = wide_filt[...].reshape(ctx, chans, tokens).astype(BF16)
    scatter(lag_send, lag_recv, 5)
    wait_scatter(filt_recv, recv_sems, 7)
    wide_filt[...] = filt_recv[...].astype(F32).reshape(ctx * chans, tokens)
    spectra(wide_filt, chans, 0, filt_spec)
    filt_real, filt_imag = parts(filt_spec)
    gate_real, gate_imag = parts(gate_spec)
    inverse(
        gate_real * filt_real - gate_imag * filt_imag,
        gate_real * filt_imag + gate_imag * filt_real,
        wide,
        2 * chans,
        0,
    )
    filt_real, filt_imag = parts(filt_spec)
    grad_real, grad_imag = parts(grad_spec)
    inverse(
        grad_real * filt_real + grad_imag * filt_imag,
        grad_imag * filt_real - grad_real * filt_imag,
        wide,
        2 * chans,
        chans,
    )
    conv_send[...] = wide[...].reshape(ctx, 2 * chans, tokens).astype(BF16)
    scatter(conv_send, conv_recv, 4)
    wait_scatter(lag_recv, recv_sems, 5)
    part_copy = remote(lag_recv, part_recv, 3, {"dp": partner})
    part_copy.start()

    wait_scatter(conv_recv, recv_sems, 4)
    both = conv_recv[...].astype(F32)
    conv = both[:, :chans].reshape(width, tokens).T
    back = both[:, chans:].reshape(width, tokens).T
    conv_out[...] = conv.astype(BF16)
    back_out[...] = back.astype(BF16)

    def rounded(x):
        return x.astype(BF16).astype(F32)

    head = 16
    after_send[0, 0:2] = rounded(grad_ref[:head].astype(F32) * conv[:head])[:2]
    after_send[0, 2:4] = rounded(vf_out[:head].astype(F32) * back[:head])[:2]
    after_send[0, 4:6] = rounded(kf_out[:head].astype(F32) * back[:head])[:2]
    after_send[0, 6:8] = jnp.zeros((2, width), F32)
    after_copy = remote(after_send, after_recv, 6, {"context": previous})
    after_copy.start()
    part_copy.wait()
    lag_sum = lag_recv[...].astype(F32) + part_recv[...].astype(F32)
    lag_out[...] = lag_sum.reshape(width, tokens).T.astype(BF16)
    after_copy.wait()
    after_out[...] = after_recv[0] * jnp.where(me == ctx - 1, 0.0, 1.0).astype(F32)
    wait_scatter(filt_mid, send_sems, 1)
    wait_scatter(filt_recv, send_sems, 7)
    wait_scatter(pair_send, send_sems, 2)
    wait_scatter(conv_send, send_sems, 4)
    wait_scatter(lag_send, send_sems, 5)


def final_kernel(
    conv_ref,
    back_ref,
    lag_ref,
    grad_ref,
    qf_ref,
    kf_ref,
    vf_ref,
    after_ref,
    taps_ref,
    out_ref,
    gq_ref,
    gk_ref,
    gv_ref,
    lag_out,
    ext,
):
    tokens = conv_ref.shape[0]
    conv = conv_ref[...].astype(F32)
    back = back_ref[...].astype(F32)
    out_ref[0] = (qf_ref[...].astype(F32) * conv).astype(BF16)

    def unfeatured(rows, which, dest):
        ext[0:tokens] = rows.astype(BF16).astype(F32)
        ext[tokens : tokens + 2] = after_ref[2 * which : 2 * which + 2]
        total = None
        for lag in range(3):
            term = taps_ref[which, lag : lag + 1, :] * ext[lag : lag + tokens]
            total = term if total is None else total + term
        dest[0] = total.astype(BF16)

    unfeatured(grad_ref[...].astype(F32) * conv, 0, gq_ref)
    unfeatured(back * vf_ref[...].astype(F32), 1, gk_ref)
    unfeatured(back * kf_ref[...].astype(F32), 2, gv_ref)
    lag_out[...] = lag_ref[...]


def on_device(ctx, queries, key_gates, values, out_grad, featurizer, long_filter):
    tokens, width = long_filter.shape
    chans = width // ctx
    fast = 1 << ((ctx.bit_length() - 1) // 2)
    table, twist = tables(ctx, tokens)
    slow = ctx // fast
    operands = (
        long_filter,
        queries[0],
        key_gates[0],
        values[0],
        out_grad[0],
        featurizer,
        table,
        twist,
    )
    vmem = pl.BlockSpec(memory_space=pltpu.VMEM)
    like = lambda *shape, dtype=BF16: jax.ShapeDtypeStruct(shape, dtype)
    buf = lambda *shape, dtype=BF16: pltpu.VMEM(shape, dtype)
    results = pl.pallas_call(
        functools.partial(main_kernel, (ctx, chans, fast)),
        out_shape=(
            like(tokens, width),
            like(tokens, width),
            like(tokens, width),
            like(tokens, width),
            like(tokens, width),
            like(tokens, width),
            like(tokens, width),
            like(8, width, dtype=F32),
            like(*featurizer.shape, dtype=F32),
        ),
        in_specs=[pl.BlockSpec(memory_space=pltpu.HBM)] * len(operands),
        out_specs=(vmem,) * 9,
        scratch_shapes=[
            *(buf(*x.shape, dtype=x.dtype) for x in operands[:-1]),
            buf(2 * ctx, tokens, dtype=F32),
            buf(tokens + 16, width, dtype=F32),
            buf(1, 8, width, dtype=F32),
            buf(1, 8, width, dtype=F32),
            buf(1, 8, width, dtype=F32),
            buf(1, 8, width, dtype=F32),
            buf(slow, fast, chans, tokens),
            buf(fast, slow, chans, tokens),
            buf(slow, fast, chans, tokens),
            buf(ctx, 2 * chans, tokens),
            buf(ctx, 2 * chans, tokens),
            buf(ctx, chans, tokens),
            buf(ctx, 2 * chans, tokens),
            buf(ctx, 2 * chans, tokens),
            buf(ctx, chans, tokens),
            buf(ctx, chans, tokens),
            buf(ctx * 2 * chans, tokens, dtype=F32),
            buf(ctx * chans, tokens, dtype=F32),
            buf(ctx * chans, 2 * tokens),
            buf(ctx * chans, 2 * tokens, dtype=F32),
            buf(ctx * chans, 2 * tokens, dtype=F32),
            buf(ctx * chans, 2 * tokens, dtype=F32),
            buf(ctx * chans, 2 * tokens),
            pltpu.SemaphoreType.DMA((len(operands),)),
            pltpu.SemaphoreType.DMA((8,)),
            pltpu.SemaphoreType.DMA((8,)),
            pltpu.SemaphoreType.REGULAR,
        ],
        compiler_params=pltpu.CompilerParams(
            collective_id=0, has_side_effects=True, vmem_limit_bytes=GRANT
        ),
        name="exchange",
    )(*operands)
    conv, back, lag, qf, kf, vf, grad, after, taps = results
    return pl.pallas_call(
        final_kernel,
        out_shape=(like(1, tokens, width),) * 4 + (like(tokens, width),),
        in_specs=[vmem] * 9,
        out_specs=(vmem,) * 5,
        scratch_shapes=[buf(tokens + 16, width, dtype=F32)],
        compiler_params=pltpu.CompilerParams(vmem_limit_bytes=32 * 1024 * 1024),
        name="finish",
    )(conv, back, lag, grad, qf, kf, vf, after, taps)


def solution(mesh):
    in_specs = (
        P("dp", "context", "tensor"),
        P("dp", "context", "tensor"),
        P("dp", "context", "tensor"),
        P("dp", "context", "tensor"),
        P(None, None, "tensor"),
        P("context", "tensor"),
    )
    out_specs = (
        P("dp", "context", "tensor"),
        P("dp", "context", "tensor"),
        P("dp", "context", "tensor"),
        P("dp", "context", "tensor"),
        P("context", "tensor"),
    )
    return jax.shard_map(
        functools.partial(on_device, mesh.shape["context"]),
        mesh=mesh,
        in_specs=in_specs,
        out_specs=out_specs,
        check_vma=False,
    )
```

```python
import functools
import math

import ml_dtypes
import numpy as np

import jax
import jax.numpy as jnp
from jax import lax
from jax.experimental import pallas as pl
from jax.experimental.pallas import tpu as pltpu
from jax.sharding import PartitionSpec as P

MESH = pl.DeviceIdType.MESH
F32 = jnp.float32
BF16 = jnp.bfloat16
GRANT = 40000 * 1024


def tables(blocks, width):
    full = 2 * blocks * width
    a = np.arange(blocks) + 0.5
    q = np.arange(blocks)
    p = np.arange(width)
    angle_qa = 2.0 * math.pi * np.outer(a, q) / (2 * blocks)
    first = np.concatenate([np.cos(angle_qa), -np.sin(angle_qa)], axis=0)
    last = np.concatenate([np.cos(angle_qa.T), -np.sin(angle_qa.T)], axis=1) * (2.0 / full)
    angle_ap = 2.0 * math.pi * np.outer(a, p) / full
    twist = np.stack([np.cos(angle_ap), np.sin(angle_ap)])
    angle_pb = 2.0 * math.pi * (np.outer(p, p) % width) / width
    cos, sin = np.cos(angle_pb), np.sin(angle_pb)
    middle = np.block([[cos, -sin], [sin, cos]])
    half = np.zeros((2 * 2 * width + 2 * blocks + blocks, 2 * width), np.float32)
    half[: 2 * width] = middle
    half[2 * width : 4 * width] = middle.T
    half[4 * width : 4 * width + 2 * blocks, :blocks] = first
    half[4 * width + 2 * blocks :, : 2 * blocks] = last
    wide = np.zeros((8 * blocks, width), np.float32)
    wide[: 2 * blocks] = twist.reshape(2 * blocks, width)
    return jnp.asarray(half.astype(ml_dtypes.bfloat16)), jnp.asarray(wide)


def far_first(step, count):
    up = (step + 1) // 2
    return lax.rem(count // 2 + jnp.where(lax.rem(step, 2) == 1, up, count - step // 2), count)


def main_kernel(
    sizes,
    filt_hbm,
    query_hbm,
    key_hbm,
    value_hbm,
    grad_hbm,
    feat_hbm,
    table_hbm,
    twist_hbm,
    conv_out,
    back_out,
    lag_out,
    qf_out,
    kf_out,
    vf_out,
    grad_out,
    after_out,
    taps,
    filt_ref,
    query_ref,
    key_ref,
    value_ref,
    grad_ref,
    feat_ref,
    table_ref,
    twist_ref,
    ext,
    rim_send,
    rim_recv,
    head_send,
    head_recv,
    feat_next,
    heads_send,
    heads_recv,
    filt_send,
    filt_mid,
    filt_recv,
    pair_send,
    pair_recv,
    part_recv,
    conv_send,
    conv_recv,
    lag_send,
    lag_recv,
    wide,
    wide_filt,
    turned,
    filt_spec,
    gate_spec,
    grad_spec,
    product,
    load_sems,
    send_sems,
    recv_sems,
    ring_sem,
):
    ctx, chans, fast = sizes
    tokens, width = query_ref.shape
    middle_rows, back_rows = pl.ds(0, 2 * tokens), pl.ds(2 * tokens, 2 * tokens)
    first_rows, last_rows = pl.ds(4 * tokens, 2 * ctx), pl.ds(4 * tokens + 2 * ctx, ctx)
    me = lax.axis_index("context")
    dp = lax.axis_index("dp")
    slow = ctx // fast
    my_slow, my_fast = me // fast, lax.rem(me, fast)
    following, previous = lax.rem(me + 1, ctx), lax.rem(me + ctx - 1, ctx)
    partner = 1 - dp

    barrier = pltpu.get_barrier_semaphore()

    def peer_of(step):
        s, f = far_first(step // fast, slow), far_first(lax.rem(step, fast), fast)
        return lax.rem(my_slow + s, slow) * fast + lax.rem(my_fast + f, fast)

    def tell(sem, device):
        pl.semaphore_signal(sem, inc=1, device_id=device, device_id_type=MESH)

    def in_slow_ring(step):
        return lax.rem(my_slow + far_first(step, slow), slow) * fast + my_fast

    def in_fast_ring(step):
        return my_slow * fast + lax.rem(my_fast + far_first(step, fast), fast)

    @pl.loop(0, slow - 1)
    def _(step):
        tell(barrier, {"context": in_slow_ring(step)})

    @pl.loop(0, fast - 1)
    def _(step):
        tell(barrier, {"context": in_fast_ring(step)})

    tell(barrier, {"context": following})
    tell(barrier, {"context": previous})
    tell(barrier, {"dp": partner})

    loads = [
        pltpu.make_async_copy(src, dst, load_sems.at[i])
        for i, (src, dst) in enumerate(
            (
                (query_hbm, query_ref),
                (key_hbm, key_ref),
                (value_hbm, value_ref),
                (feat_hbm, feat_ref),
                (grad_hbm, grad_ref),
                (filt_hbm, filt_ref),
                (table_hbm, table_ref),
                (twist_hbm.at[pl.ds(0, 2 * ctx)], twist_ref),
            )
        )
    ]
    for load in loads:
        load.start()

    def remote(src, dst, which, device):
        return pltpu.make_async_remote_copy(
            src_ref=src,
            dst_ref=dst,
            send_sem=send_sems.at[which],
            recv_sem=recv_sems.at[which],
            device_id=device,
            device_id_type=MESH,
        )

    def scatter(src, dst, which, with_heads=False):
        @pl.loop(0, ctx - 1)
        def _(step):
            peer = peer_of(step)
            remote(src.at[peer], dst.at[me], which, {"context": peer}).start()
            if with_heads:
                after = lax.rem(peer + 1, ctx)
                remote(heads_send.at[after], heads_recv.at[me], 8, {"context": peer}).start()

        dst[me] = src[me]
        if with_heads:
            heads_recv[me] = heads_send[following]

    def ring_scatter(src, dst, place, mine, count, which):
        @pl.loop(0, count - 1)
        def _(step):
            at = lax.rem(mine + far_first(step, count), count)
            remote(src.at[:, at], dst.at[mine], which, {"context": place(step)}).start()

        dst[mine] = src[:, mine]

    def wait_scatter(ref, sems, which):
        rows = ref.at[pl.ds(0, ref.shape[0] - 1)]
        pltpu.make_async_copy(rows, rows, sems.at[which]).wait()

    for load in loads[:3]:
        load.wait()
    for row, rows_ref in enumerate((query_ref, key_ref, value_ref)):
        rim_send[0, 2 * row : 2 * row + 2] = rows_ref[tokens - 16 :].astype(F32)[14:]
    rim_send[0, 6:8] = jnp.zeros((2, width), F32)

    for load in loads[3:]:
        load.wait()
    taps[...] = feat_ref[...].astype(F32)
    for row, rows_ref in enumerate((grad_ref, key_ref, value_ref)):
        head_send[0, 2 * row : 2 * row + 2] = rows_ref[:16].astype(F32)[:2]
    head_send[0, 6:8] = jnp.zeros((2, width), F32)
    by_channel = filt_ref[...].astype(F32).T.reshape(slow, fast, chans, tokens)
    filt_send[...] = by_channel.astype(BF16)

    pl.semaphore_wait(barrier, slow + fast + 1)

    rim_copy = remote(rim_send, rim_recv, 0, {"context": following})
    rim_copy.start()
    head_copy = remote(head_send, head_recv, 6, {"context": previous})
    head_copy.start()

    @pl.loop(0, slow - 1)
    def _(step):
        tell(ring_sem, {"context": in_slow_ring(step)})

    ring_scatter(filt_send, filt_mid, in_fast_ring, my_fast, fast, 1)
    rim_copy.wait()
    head_copy.wait()

    keep = jnp.where(me == 0, 0.0, 1.0).astype(F32)

    def featured(rows_ref, which, start=8, count=None):
        if count is None:
            count = tokens
            ext[8 : 8 + tokens] = rows_ref[...].astype(F32)
            ext[6:8] = rim_recv[0, 2 * which : 2 * which + 2] * keep
        total = None
        for lag in range(3):
            tap = taps[which, lag : lag + 1, :]
            term = tap * ext[start - lag : start - lag + count]
            total = term if total is None else total + term
        return total.astype(BF16)

    def featured_after(which):
        ext[8 + tokens : 10 + tokens] = head_recv[0, 2 * which : 2 * which + 2]
        return featured(None, which, 8 + tokens, 2).astype(F32)

    query_feat = featured(query_ref, 0)
    qf_out[...] = query_feat
    key_feat = featured(key_ref, 1)
    feat_next[0:2] = featured_after(1)
    kf_out[...] = key_feat
    value_feat = featured(value_ref, 2)
    feat_next[2:4] = featured_after(2)
    vf_out[...] = value_feat
    grad_out[...] = grad_ref[...]
    gated = (key_feat.astype(F32) * value_feat.astype(F32)).T.reshape(ctx, chans, tokens)
    signal = (grad_ref[...].astype(F32) * query_feat.astype(F32)).T.reshape(ctx, chans, tokens)
    pair_send[...] = jnp.concatenate([gated, signal], axis=1).astype(BF16)
    pl.semaphore_wait(ring_sem, slow - 1)
    scatter(pair_send, pair_recv, 2)
    wait_scatter(filt_mid, recv_sems, 1)
    ring_scatter(filt_mid, filt_recv, in_slow_ring, my_slow, slow, 7)

    def spectra(wide_ref, rows, start, dest):
        for channel in range(chans):
            grid = wide_ref[pl.ds(start + channel, ctx, stride=rows), :].astype(BF16)
            section = jnp.dot(table_ref[first_rows, 0:ctx], grid, preferred_element_type=F32)
            real, imag = section[:ctx], section[ctx:]
            cos, sin = twist_ref[0:ctx], twist_ref[ctx : 2 * ctx]
            here = pl.ds(channel * ctx, ctx)
            turned[here, 0:tokens] = (real * cos + imag * sin).astype(BF16)
            turned[here, tokens : 2 * tokens] = (imag * cos - real * sin).astype(BF16)
        dest[...] = jnp.dot(turned[...], table_ref[middle_rows], preferred_element_type=F32)

    wait_scatter(pair_recv, recv_sems, 2)
    wide[...] = pair_recv[...].astype(F32).reshape(ctx * 2 * chans, tokens)
    spectra(wide, 2 * chans, 0, gate_spec)
    spectra(wide, 2 * chans, chans, grad_spec)

    def parts(ref):
        return ref[:, 0:tokens], ref[:, tokens : 2 * tokens]

    lane = lax.broadcasted_iota(jnp.int32, (ctx, tokens), 1)

    def inverse(real, imag, wide_ref, rows, start, heads=None):
        product[:, 0:tokens] = real.astype(BF16)
        product[:, tokens : 2 * tokens] = imag.astype(BF16)
        gate = jnp.dot(product[...], table_ref[back_rows], preferred_element_type=F32)
        cos, sin = twist_ref[0:ctx], twist_ref[ctx : 2 * ctx]
        for channel in range(chans):
            piece = gate[channel * ctx : (channel + 1) * ctx]
            real, imag = piece[:, :tokens], piece[:, tokens:]
            stacked = jnp.concatenate([real * cos - imag * sin, imag * cos + real * sin], axis=0)
            result = jnp.dot(
                table_ref[last_rows, 0 : 2 * ctx], stacked.astype(BF16), preferred_element_type=F32
            )
            wide_ref[pl.ds(start + channel, ctx, stride=rows), :] = result
            if heads is not None:
                head = jnp.where(lane < 2, result, 0.0)
                heads.append(pltpu.roll(head, 2 * (start + channel), 1))

    gate_real, gate_imag = parts(gate_spec)
    grad_real, grad_imag = parts(grad_spec)
    inverse(
        grad_real * gate_real + grad_imag * gate_imag,
        grad_imag * gate_real - grad_real * gate_imag,
        wide_filt,
        chans,
        0,
    )
    lag_send[...] = wide_filt[...].reshape(ctx, chans, tokens).astype(BF16)
    scatter(lag_send, lag_recv, 5)
    wait_scatter(filt_recv, recv_sems, 7)
    heads = []
    wide_filt[...] = filt_recv[...].astype(F32).reshape(ctx * chans, tokens)
    spectra(wide_filt, chans, 0, filt_spec)
    filt_real, filt_imag = parts(filt_spec)
    gate_real, gate_imag = parts(gate_spec)
    inverse(
        gate_real * filt_real - gate_imag * filt_imag,
        gate_real * filt_imag + gate_imag * filt_real,
        wide,
        2 * chans,
        0,
        heads,
    )
    filt_real, filt_imag = parts(filt_spec)
    grad_real, grad_imag = parts(grad_spec)
    inverse(
        grad_real * filt_real + grad_imag * filt_imag,
        grad_imag * filt_real - grad_real * filt_imag,
        wide,
        2 * chans,
        chans,
        heads,
    )
    heads_send[...] = sum(heads).reshape(ctx, 1, tokens)
    conv_send[...] = wide[...].reshape(ctx, 2 * chans, tokens).astype(BF16)
    scatter(conv_send, conv_recv, 4, True)
    wait_scatter(lag_recv, recv_sems, 5)
    part_copy = remote(lag_recv, part_recv, 3, {"dp": partner})
    part_copy.start()

    wait_scatter(conv_recv, recv_sems, 4)
    both = conv_recv[...].astype(F32)
    conv = both[:, :chans].reshape(width, tokens).T
    back = both[:, chans:].reshape(width, tokens).T
    conv_out[...] = conv.astype(BF16)
    back_out[...] = back.astype(BF16)

    def rounded(x):
        return x.astype(BF16).astype(F32)

    wait_scatter(heads_recv, recv_sems, 8)
    packed = heads_recv[...].reshape(ctx, tokens).astype(BF16)
    from_lane = lax.broadcasted_iota(jnp.int32, (tokens, width), 0)
    to_chan = lax.broadcasted_iota(jnp.int32, (tokens, width), 1) % chans
    holder = lax.broadcasted_iota(jnp.int32, (ctx, width), 0)
    is_mine = lax.broadcasted_iota(jnp.int32, (ctx, width), 1) // chans == holder

    def next_row(kind, position):
        pick = from_lane == 2 * (to_chan + chans * kind) + position
        spread = jnp.dot(packed, jnp.where(pick, 1.0, 0.0).astype(BF16), preferred_element_type=F32)
        return jnp.sum(jnp.where(is_mine, spread, 0.0), axis=0, keepdims=True)

    last_keep = jnp.where(me == ctx - 1, 0.0, 1.0).astype(F32)
    for position in range(2):
        conv_next, back_next = next_row(0, position), next_row(1, position)
        at = slice(position, position + 1)
        after_out[at] = rounded(head_recv[0, at] * conv_next) * last_keep
        at = slice(2 + position, 3 + position)
        after_out[at] = rounded(feat_next[at] * back_next) * last_keep
        into = slice(4 + position, 5 + position)
        after_out[into] = rounded(feat_next[slice(position, position + 1)] * back_next) * last_keep
    after_out[6:8] = jnp.zeros((2, width), F32)
    part_copy.wait()
    lag_sum = lag_recv[...].astype(F32) + part_recv[...].astype(F32)
    lag_out[...] = lag_sum.reshape(width, tokens).T.astype(BF16)
    wait_scatter(heads_send, send_sems, 8)
    wait_scatter(filt_mid, send_sems, 1)
    wait_scatter(filt_recv, send_sems, 7)
    wait_scatter(pair_send, send_sems, 2)
    wait_scatter(conv_send, send_sems, 4)
    wait_scatter(lag_send, send_sems, 5)


def final_kernel(
    conv_ref,
    back_ref,
    lag_ref,
    grad_ref,
    qf_ref,
    kf_ref,
    vf_ref,
    after_ref,
    taps_ref,
    out_ref,
    gq_ref,
    gk_ref,
    gv_ref,
    lag_out,
    ext,
):
    tokens = conv_ref.shape[0]
    conv = conv_ref[...].astype(F32)
    back = back_ref[...].astype(F32)
    out_ref[0] = (qf_ref[...].astype(F32) * conv).astype(BF16)

    def unfeatured(rows, which, dest):
        ext[0:tokens] = rows.astype(BF16).astype(F32)
        ext[tokens : tokens + 2] = after_ref[2 * which : 2 * which + 2]
        total = None
        for lag in range(3):
            term = taps_ref[which, lag : lag + 1, :] * ext[lag : lag + tokens]
            total = term if total is None else total + term
        dest[0] = total.astype(BF16)

    unfeatured(grad_ref[...].astype(F32) * conv, 0, gq_ref)
    unfeatured(back * vf_ref[...].astype(F32), 1, gk_ref)
    unfeatured(back * kf_ref[...].astype(F32), 2, gv_ref)
    lag_out[...] = lag_ref[...]


def on_device(ctx, queries, key_gates, values, out_grad, featurizer, long_filter):
    tokens, width = long_filter.shape
    chans = width // ctx
    fast = 1 << ((ctx.bit_length() - 1) // 2)
    table, twist = tables(ctx, tokens)
    slow = ctx // fast
    operands = (
        long_filter,
        queries[0],
        key_gates[0],
        values[0],
        out_grad[0],
        featurizer,
        table,
        twist,
    )
    vmem = pl.BlockSpec(memory_space=pltpu.VMEM)
    like = lambda *shape, dtype=BF16: jax.ShapeDtypeStruct(shape, dtype)
    buf = lambda *shape, dtype=BF16: pltpu.VMEM(shape, dtype)
    results = pl.pallas_call(
        functools.partial(main_kernel, (ctx, chans, fast)),
        out_shape=(
            like(tokens, width),
            like(tokens, width),
            like(tokens, width),
            like(tokens, width),
            like(tokens, width),
            like(tokens, width),
            like(tokens, width),
            like(8, width, dtype=F32),
            like(*featurizer.shape, dtype=F32),
        ),
        in_specs=[pl.BlockSpec(memory_space=pltpu.HBM)] * len(operands),
        out_specs=(vmem,) * 9,
        scratch_shapes=[
            *(buf(*x.shape, dtype=x.dtype) for x in operands[:-1]),
            buf(2 * ctx, tokens, dtype=F32),
            buf(tokens + 16, width, dtype=F32),
            buf(1, 8, width, dtype=F32),
            buf(1, 8, width, dtype=F32),
            buf(1, 8, width, dtype=F32),
            buf(1, 8, width, dtype=F32),
            buf(8, width, dtype=F32),
            buf(ctx, 1, tokens, dtype=F32),
            buf(ctx, 1, tokens, dtype=F32),
            buf(slow, fast, chans, tokens),
            buf(fast, slow, chans, tokens),
            buf(slow, fast, chans, tokens),
            buf(ctx, 2 * chans, tokens),
            buf(ctx, 2 * chans, tokens),
            buf(ctx, chans, tokens),
            buf(ctx, 2 * chans, tokens),
            buf(ctx, 2 * chans, tokens),
            buf(ctx, chans, tokens),
            buf(ctx, chans, tokens),
            buf(ctx * 2 * chans, tokens, dtype=F32),
            buf(ctx * chans, tokens, dtype=F32),
            buf(ctx * chans, 2 * tokens),
            buf(ctx * chans, 2 * tokens, dtype=F32),
            buf(ctx * chans, 2 * tokens, dtype=F32),
            buf(ctx * chans, 2 * tokens, dtype=F32),
            buf(ctx * chans, 2 * tokens),
            pltpu.SemaphoreType.DMA((len(operands),)),
            pltpu.SemaphoreType.DMA((9,)),
            pltpu.SemaphoreType.DMA((9,)),
            pltpu.SemaphoreType.REGULAR,
        ],
        compiler_params=pltpu.CompilerParams(
            collective_id=0, has_side_effects=True, vmem_limit_bytes=GRANT
        ),
        name="exchange",
    )(*(pltpu.with_memory_space_constraint(x, pltpu.HBM) for x in operands))
    conv, back, lag, qf, kf, vf, grad, after, taps = results
    return pl.pallas_call(
        final_kernel,
        out_shape=(like(1, tokens, width),) * 4 + (like(tokens, width),),
        in_specs=[vmem] * 9,
        out_specs=(vmem,) * 5,
        scratch_shapes=[buf(tokens + 16, width, dtype=F32)],
        compiler_params=pltpu.CompilerParams(vmem_limit_bytes=32 * 1024 * 1024),
        name="finish",
    )(conv, back, lag, grad, qf, kf, vf, after, taps)


def solution(mesh):
    in_specs = (
        P("dp", "context", "tensor"),
        P("dp", "context", "tensor"),
        P("dp", "context", "tensor"),
        P("dp", "context", "tensor"),
        P(None, None, "tensor"),
        P("context", "tensor"),
    )
    out_specs = (
        P("dp", "context", "tensor"),
        P("dp", "context", "tensor"),
        P("dp", "context", "tensor"),
        P("dp", "context", "tensor"),
        P("context", "tensor"),
    )
    return jax.shard_map(
        functools.partial(on_device, mesh.shape["context"]),
        mesh=mesh,
        in_specs=in_specs,
        out_specs=out_specs,
        check_vma=False,
    )
```

```python
import functools
import math

import ml_dtypes
import numpy as np

import jax
import jax.numpy as jnp
from jax import lax
from jax.experimental import pallas as pl
from jax.experimental.pallas import tpu as pltpu
from jax.sharding import PartitionSpec as P

MESH = pl.DeviceIdType.MESH
F32 = jnp.float32
BF16 = jnp.bfloat16
GRANT = 40000 * 1024


def tables(blocks, width):
    full = 2 * blocks * width
    a = np.arange(blocks) + 0.5
    q = np.arange(blocks)
    p = np.arange(width)
    angle_qa = 2.0 * math.pi * np.outer(a, q) / (2 * blocks)
    first = np.concatenate([np.cos(angle_qa), -np.sin(angle_qa)], axis=0)
    last = np.concatenate([np.cos(angle_qa.T), -np.sin(angle_qa.T)], axis=1) * (2.0 / full)
    angle_ap = 2.0 * math.pi * np.outer(a, p) / full
    twist = np.stack([np.cos(angle_ap), np.sin(angle_ap)])
    angle_pb = 2.0 * math.pi * (np.outer(p, p) % width) / width
    cos, sin = np.cos(angle_pb), np.sin(angle_pb)
    middle = np.block([[cos, -sin], [sin, cos]])
    half = np.zeros((2 * 2 * width + 2 * blocks + blocks, 2 * width), np.float32)
    half[: 2 * width] = middle
    half[2 * width : 4 * width] = middle.T
    half[4 * width : 4 * width + 2 * blocks, :blocks] = first
    half[4 * width + 2 * blocks :, : 2 * blocks] = last
    wide = np.zeros((8 * blocks, width), np.float32)
    wide[: 2 * blocks] = twist.reshape(2 * blocks, width)
    return jnp.asarray(half.astype(ml_dtypes.bfloat16)), jnp.asarray(wide)


def far_first(step, count):
    up = (step + 1) // 2
    return lax.rem(count // 2 + jnp.where(lax.rem(step, 2) == 1, up, count - step // 2), count)


def far_offsets(count):
    return [(count // 2 + ((i + 1) // 2 if i % 2 else -(i // 2))) % count for i in range(count)]


def main_kernel(
    sizes,
    filt_hbm,
    query_hbm,
    key_hbm,
    value_hbm,
    grad_hbm,
    feat_hbm,
    table_hbm,
    twist_hbm,
    conv_out,
    back_out,
    lag_out,
    qf_out,
    kf_out,
    vf_out,
    grad_out,
    after_out,
    taps,
    filt_ref,
    query_ref,
    key_ref,
    value_ref,
    grad_ref,
    feat_ref,
    table_ref,
    twist_ref,
    ext,
    rim_send,
    rim_recv,
    head_send,
    head_recv,
    feat_next,
    heads_send,
    heads_recv,
    filt_send,
    filt_mid,
    filt_recv,
    pair_send,
    pair_recv,
    part_recv,
    conv_send,
    conv_recv,
    lag_send,
    lag_recv,
    wide,
    wide_filt,
    turned,
    filt_spec,
    gate_spec,
    grad_spec,
    product,
    load_sems,
    send_sems,
    recv_sems,
    ring_sem,
):
    ctx, chans, fast = sizes
    tokens, width = query_ref.shape
    middle_rows, back_rows = pl.ds(0, 2 * tokens), pl.ds(2 * tokens, 2 * tokens)
    first_rows, last_rows = pl.ds(4 * tokens, 2 * ctx), pl.ds(4 * tokens + 2 * ctx, ctx)
    me = lax.axis_index("context")
    dp = lax.axis_index("dp")
    slow = ctx // fast
    my_slow, my_fast = me // fast, lax.rem(me, fast)
    following, previous = lax.rem(me + 1, ctx), lax.rem(me + ctx - 1, ctx)
    partner = 1 - dp

    barrier = pltpu.get_barrier_semaphore()

    def tell(sem, device):
        pl.semaphore_signal(sem, inc=1, device_id=device, device_id_type=MESH)

    def in_slow_ring(step):
        return lax.rem(my_slow + far_first(step, slow), slow) * fast + my_fast

    def in_fast_ring(step):
        return my_slow * fast + lax.rem(my_fast + far_first(step, fast), fast)

    @pl.loop(0, slow - 1)
    def _(step):
        tell(barrier, {"context": in_slow_ring(step)})

    @pl.loop(0, fast - 1)
    def _(step):
        tell(barrier, {"context": in_fast_ring(step)})

    tell(barrier, {"context": following})
    tell(barrier, {"context": previous})
    tell(barrier, {"dp": partner})

    loads = [
        pltpu.make_async_copy(src, dst, load_sems.at[i])
        for i, (src, dst) in enumerate(
            (
                (query_hbm, query_ref),
                (key_hbm, key_ref),
                (value_hbm, value_ref),
                (feat_hbm, feat_ref),
                (grad_hbm, grad_ref),
                (filt_hbm, filt_ref),
                (table_hbm, table_ref),
                (twist_hbm.at[pl.ds(0, 2 * ctx)], twist_ref),
            )
        )
    ]
    for load in loads:
        load.start()

    def remote(src, dst, which, device):
        return pltpu.make_async_remote_copy(
            src_ref=src,
            dst_ref=dst,
            send_sem=send_sems.at[which],
            recv_sem=recv_sems.at[which],
            device_id=device,
            device_id_type=MESH,
        )

    fast_places = [lax.rem(my_fast + offset, fast) for offset in far_offsets(fast)]

    def scatter(src, dst, which, with_heads=False):
        def send_row(row, count):
            base = row * fast
            for place in fast_places[:count]:
                peer = base + place
                remote(src.at[peer], dst.at[me], which, {"context": peer}).start()
                if with_heads:
                    remote(heads_send.at[peer], heads_recv.at[me], 8, {"context": peer}).start()

        @pl.loop(0, slow - 1)
        def _(step):
            send_row(lax.rem(my_slow + far_first(step, slow), slow), fast)

        send_row(my_slow, fast - 1)
        dst[me] = src[me]
        if with_heads:
            heads_recv[me] = heads_send[me]

    def ring_scatter(src, dst, place, mine, count, which):
        @pl.loop(0, count - 1)
        def _(step):
            at = lax.rem(mine + far_first(step, count), count)
            remote(src.at[:, at], dst.at[mine], which, {"context": place(step)}).start()

        dst[mine] = src[:, mine]

    def wait_scatter(ref, sems, which):
        rows = ref.at[pl.ds(0, ref.shape[0] - 1)]
        pltpu.make_async_copy(rows, rows, sems.at[which]).wait()

    for load in loads[:3]:
        load.wait()
    for row, rows_ref in enumerate((query_ref, key_ref, value_ref)):
        rim_send[0, 2 * row : 2 * row + 2] = rows_ref[tokens - 16 :].astype(F32)[14:]
    rim_send[0, 6:8] = jnp.zeros((2, width), F32)

    for load in loads[3:]:
        load.wait()
    taps[...] = feat_ref[...].astype(F32)
    for row, rows_ref in enumerate((grad_ref, key_ref, value_ref)):
        head_send[0, 2 * row : 2 * row + 2] = rows_ref[:16].astype(F32)[:2]
    head_send[0, 6:8] = jnp.zeros((2, width), F32)
    by_channel = filt_ref[...].astype(F32).T.reshape(slow, fast, chans, tokens)
    filt_send[...] = by_channel.astype(BF16)

    pl.semaphore_wait(barrier, slow + fast + 1)

    rim_copy = remote(rim_send, rim_recv, 0, {"context": following})
    rim_copy.start()
    head_copy = remote(head_send, head_recv, 6, {"context": previous})
    head_copy.start()

    @pl.loop(0, slow - 1)
    def _(step):
        tell(ring_sem, {"context": in_slow_ring(step)})

    ring_scatter(filt_send, filt_mid, in_fast_ring, my_fast, fast, 1)
    rim_copy.wait()
    head_copy.wait()

    keep = jnp.where(me == 0, 0.0, 1.0).astype(F32)

    def featured(rows_ref, which, start=8, count=None):
        if count is None:
            count = tokens
            ext[8 : 8 + tokens] = rows_ref[...].astype(F32)
            ext[6:8] = rim_recv[0, 2 * which : 2 * which + 2] * keep
        total = None
        for lag in range(3):
            tap = taps[which, lag : lag + 1, :]
            term = tap * ext[start - lag : start - lag + count]
            total = term if total is None else total + term
        return total.astype(BF16)

    def featured_after(which):
        ext[8 + tokens : 10 + tokens] = head_recv[0, 2 * which : 2 * which + 2]
        return featured(None, which, 8 + tokens, 2).astype(F32)

    query_feat = featured(query_ref, 0)
    qf_out[...] = query_feat
    key_feat = featured(key_ref, 1)
    feat_next[0:2] = featured_after(1)
    kf_out[...] = key_feat
    value_feat = featured(value_ref, 2)
    feat_next[2:4] = featured_after(2)
    vf_out[...] = value_feat
    grad_out[...] = grad_ref[...]
    gated = (key_feat.astype(F32) * value_feat.astype(F32)).T.reshape(ctx, chans, tokens)
    signal = (grad_ref[...].astype(F32) * query_feat.astype(F32)).T.reshape(ctx, chans, tokens)
    pair_send[...] = jnp.concatenate([gated, signal], axis=1).astype(BF16)
    pl.semaphore_wait(ring_sem, slow - 1)
    scatter(pair_send, pair_recv, 2)
    wait_scatter(filt_mid, recv_sems, 1)
    ring_scatter(filt_mid, filt_recv, in_slow_ring, my_slow, slow, 7)

    def spectra(wide_ref, rows, start, dest):
        for channel in range(chans):
            grid = wide_ref[pl.ds(start + channel, ctx, stride=rows), :].astype(BF16)
            section = jnp.dot(table_ref[first_rows, 0:ctx], grid, preferred_element_type=F32)
            real, imag = section[:ctx], section[ctx:]
            cos, sin = twist_ref[0:ctx], twist_ref[ctx : 2 * ctx]
            here = pl.ds(channel * ctx, ctx)
            turned[here, 0:tokens] = (real * cos + imag * sin).astype(BF16)
            turned[here, tokens : 2 * tokens] = (imag * cos - real * sin).astype(BF16)
        dest[...] = jnp.dot(turned[...], table_ref[middle_rows], preferred_element_type=F32)

    wait_scatter(pair_recv, recv_sems, 2)
    wide[...] = pair_recv[...].astype(F32).reshape(ctx * 2 * chans, tokens)
    spectra(wide, 2 * chans, 0, gate_spec)
    spectra(wide, 2 * chans, chans, grad_spec)

    def parts(ref):
        return ref[:, 0:tokens], ref[:, tokens : 2 * tokens]

    lane = lax.broadcasted_iota(jnp.int32, (ctx, tokens), 1)

    def inverse(real, imag, wide_ref, rows, start, heads=None):
        product[:, 0:tokens] = real.astype(BF16)
        product[:, tokens : 2 * tokens] = imag.astype(BF16)
        gate = jnp.dot(product[...], table_ref[back_rows], preferred_element_type=F32)
        cos, sin = twist_ref[0:ctx], twist_ref[ctx : 2 * ctx]
        for channel in range(chans):
            piece = gate[channel * ctx : (channel + 1) * ctx]
            real, imag = piece[:, :tokens], piece[:, tokens:]
            stacked = jnp.concatenate([real * cos - imag * sin, imag * cos + real * sin], axis=0)
            result = jnp.dot(
                table_ref[last_rows, 0 : 2 * ctx], stacked.astype(BF16), preferred_element_type=F32
            )
            wide_ref[pl.ds(start + channel, ctx, stride=rows), :] = result
            if heads is not None:
                head = jnp.where(lane < 2, result, 0.0)
                heads.append(pltpu.roll(head, 2 * (start + channel), 1))

    gate_real, gate_imag = parts(gate_spec)
    grad_real, grad_imag = parts(grad_spec)
    inverse(
        grad_real * gate_real + grad_imag * gate_imag,
        grad_imag * gate_real - grad_real * gate_imag,
        wide_filt,
        chans,
        0,
    )
    lag_send[...] = wide_filt[...].reshape(ctx, chans, tokens).astype(BF16)
    scatter(lag_send, lag_recv, 5)
    wait_scatter(filt_recv, recv_sems, 7)
    heads = []
    wide_filt[...] = filt_recv[...].astype(F32).reshape(ctx * chans, tokens)
    spectra(wide_filt, chans, 0, filt_spec)
    filt_real, filt_imag = parts(filt_spec)
    gate_real, gate_imag = parts(gate_spec)
    inverse(
        gate_real * filt_real - gate_imag * filt_imag,
        gate_real * filt_imag + gate_imag * filt_real,
        wide,
        2 * chans,
        0,
        heads,
    )
    filt_real, filt_imag = parts(filt_spec)
    grad_real, grad_imag = parts(grad_spec)
    inverse(
        grad_real * filt_real + grad_imag * filt_imag,
        grad_imag * filt_real - grad_real * filt_imag,
        wide,
        2 * chans,
        chans,
        heads,
    )
    heads_send[...] = pltpu.roll(sum(heads), ctx - 1, 0).reshape(ctx, 1, tokens)
    conv_send[...] = wide[...].reshape(ctx, 2 * chans, tokens).astype(BF16)
    scatter(conv_send, conv_recv, 4, True)
    wait_scatter(lag_recv, recv_sems, 5)
    part_copy = remote(lag_recv, part_recv, 3, {"dp": partner})
    part_copy.start()

    wait_scatter(conv_recv, recv_sems, 4)
    both = conv_recv[...].astype(F32)
    conv = both[:, :chans].reshape(width, tokens).T
    back = both[:, chans:].reshape(width, tokens).T
    conv_out[...] = conv.astype(BF16)
    back_out[...] = back.astype(BF16)

    def rounded(x):
        return x.astype(BF16).astype(F32)

    wait_scatter(heads_recv, recv_sems, 8)
    packed = heads_recv[...].reshape(ctx, tokens).astype(BF16)
    from_lane = lax.broadcasted_iota(jnp.int32, (tokens, width), 0)
    to_chan = lax.broadcasted_iota(jnp.int32, (tokens, width), 1) % chans
    holder = lax.broadcasted_iota(jnp.int32, (ctx, width), 0)
    is_mine = lax.broadcasted_iota(jnp.int32, (ctx, width), 1) // chans == holder

    def next_row(kind, position):
        pick = from_lane == 2 * (to_chan + chans * kind) + position
        spread = jnp.dot(packed, jnp.where(pick, 1.0, 0.0).astype(BF16), preferred_element_type=F32)
        return jnp.sum(jnp.where(is_mine, spread, 0.0), axis=0, keepdims=True)

    last_keep = jnp.where(me == ctx - 1, 0.0, 1.0).astype(F32)
    for position in range(2):
        conv_next, back_next = next_row(0, position), next_row(1, position)
        at = slice(position, position + 1)
        after_out[at] = rounded(head_recv[0, at] * conv_next) * last_keep
        at = slice(2 + position, 3 + position)
        after_out[at] = rounded(feat_next[at] * back_next) * last_keep
        into = slice(4 + position, 5 + position)
        after_out[into] = rounded(feat_next[slice(position, position + 1)] * back_next) * last_keep
    after_out[6:8] = jnp.zeros((2, width), F32)
    part_copy.wait()
    lag_sum = lag_recv[...].astype(F32) + part_recv[...].astype(F32)
    lag_out[...] = lag_sum.reshape(width, tokens).T.astype(BF16)
    wait_scatter(heads_send, send_sems, 8)
    wait_scatter(filt_mid, send_sems, 1)
    wait_scatter(filt_recv, send_sems, 7)
    wait_scatter(pair_send, send_sems, 2)
    wait_scatter(conv_send, send_sems, 4)
    wait_scatter(lag_send, send_sems, 5)


def final_kernel(
    conv_ref,
    back_ref,
    lag_ref,
    grad_ref,
    qf_ref,
    kf_ref,
    vf_ref,
    after_ref,
    taps_ref,
    out_ref,
    gq_ref,
    gk_ref,
    gv_ref,
    lag_out,
    ext,
):
    tokens = conv_ref.shape[0]
    conv = conv_ref[...].astype(F32)
    back = back_ref[...].astype(F32)
    out_ref[0] = (qf_ref[...].astype(F32) * conv).astype(BF16)

    def unfeatured(rows, which, dest):
        ext[0:tokens] = rows.astype(BF16).astype(F32)
        ext[tokens : tokens + 2] = after_ref[2 * which : 2 * which + 2]
        total = None
        for lag in range(3):
            term = taps_ref[which, lag : lag + 1, :] * ext[lag : lag + tokens]
            total = term if total is None else total + term
        dest[0] = total.astype(BF16)

    unfeatured(grad_ref[...].astype(F32) * conv, 0, gq_ref)
    unfeatured(back * vf_ref[...].astype(F32), 1, gk_ref)
    unfeatured(back * kf_ref[...].astype(F32), 2, gv_ref)
    lag_out[...] = lag_ref[...]


def on_device(ctx, queries, key_gates, values, out_grad, featurizer, long_filter):
    tokens, width = long_filter.shape
    chans = width // ctx
    fast = 1 << ((ctx.bit_length() - 1) // 2)
    table, twist = tables(ctx, tokens)
    slow = ctx // fast
    operands = (
        long_filter,
        queries[0],
        key_gates[0],
        values[0],
        out_grad[0],
        featurizer,
        table,
        twist,
    )
    vmem = pl.BlockSpec(memory_space=pltpu.VMEM)
    like = lambda *shape, dtype=BF16: jax.ShapeDtypeStruct(shape, dtype)
    buf = lambda *shape, dtype=BF16: pltpu.VMEM(shape, dtype)
    results = pl.pallas_call(
        functools.partial(main_kernel, (ctx, chans, fast)),
        out_shape=(
            like(tokens, width),
            like(tokens, width),
            like(tokens, width),
            like(tokens, width),
            like(tokens, width),
            like(tokens, width),
            like(tokens, width),
            like(8, width, dtype=F32),
            like(*featurizer.shape, dtype=F32),
        ),
        in_specs=[pl.BlockSpec(memory_space=pltpu.HBM)] * len(operands),
        out_specs=(vmem,) * 9,
        scratch_shapes=[
            *(buf(*x.shape, dtype=x.dtype) for x in operands[:-1]),
            buf(2 * ctx, tokens, dtype=F32),
            buf(tokens + 16, width, dtype=F32),
            buf(1, 8, width, dtype=F32),
            buf(1, 8, width, dtype=F32),
            buf(1, 8, width, dtype=F32),
            buf(1, 8, width, dtype=F32),
            buf(8, width, dtype=F32),
            buf(ctx, 1, tokens, dtype=F32),
            buf(ctx, 1, tokens, dtype=F32),
            buf(slow, fast, chans, tokens),
            buf(fast, slow, chans, tokens),
            buf(slow, fast, chans, tokens),
            buf(ctx, 2 * chans, tokens),
            buf(ctx, 2 * chans, tokens),
            buf(ctx, chans, tokens),
            buf(ctx, 2 * chans, tokens),
            buf(ctx, 2 * chans, tokens),
            buf(ctx, chans, tokens),
            buf(ctx, chans, tokens),
            buf(ctx * 2 * chans, tokens, dtype=F32),
            buf(ctx * chans, tokens, dtype=F32),
            buf(ctx * chans, 2 * tokens),
            buf(ctx * chans, 2 * tokens, dtype=F32),
            buf(ctx * chans, 2 * tokens, dtype=F32),
            buf(ctx * chans, 2 * tokens, dtype=F32),
            buf(ctx * chans, 2 * tokens),
            pltpu.SemaphoreType.DMA((len(operands),)),
            pltpu.SemaphoreType.DMA((9,)),
            pltpu.SemaphoreType.DMA((9,)),
            pltpu.SemaphoreType.REGULAR,
        ],
        compiler_params=pltpu.CompilerParams(
            collective_id=0, has_side_effects=True, vmem_limit_bytes=GRANT
        ),
        name="exchange",
    )(*(pltpu.with_memory_space_constraint(x, pltpu.HBM) for x in operands))
    conv, back, lag, qf, kf, vf, grad, after, taps = results
    return pl.pallas_call(
        final_kernel,
        out_shape=(like(1, tokens, width),) * 4 + (like(tokens, width),),
        in_specs=[vmem] * 9,
        out_specs=(vmem,) * 5,
        scratch_shapes=[buf(tokens + 16, width, dtype=F32)],
        compiler_params=pltpu.CompilerParams(vmem_limit_bytes=32 * 1024 * 1024),
        name="finish",
    )(conv, back, lag, grad, qf, kf, vf, after, taps)


def solution(mesh):
    in_specs = (
        P("dp", "context", "tensor"),
        P("dp", "context", "tensor"),
        P("dp", "context", "tensor"),
        P("dp", "context", "tensor"),
        P(None, None, "tensor"),
        P("context", "tensor"),
    )
    out_specs = (
        P("dp", "context", "tensor"),
        P("dp", "context", "tensor"),
        P("dp", "context", "tensor"),
        P("dp", "context", "tensor"),
        P("context", "tensor"),
    )
    return jax.shard_map(
        functools.partial(on_device, mesh.shape["context"]),
        mesh=mesh,
        in_specs=in_specs,
        out_specs=out_specs,
        check_vma=False,
    )
```

```python
import functools
import math

import ml_dtypes
import numpy as np

import jax
import jax.numpy as jnp
from jax import lax
from jax.experimental import pallas as pl
from jax.experimental.pallas import tpu as pltpu
from jax.sharding import PartitionSpec as P

MESH = pl.DeviceIdType.MESH
F32 = jnp.float32
BF16 = jnp.bfloat16
GRANT = 40000 * 1024


def tables(blocks, width):
    full = 2 * blocks * width
    a = np.arange(blocks) + 0.5
    q = np.arange(blocks)
    p = np.arange(width)
    angle_qa = 2.0 * math.pi * np.outer(a, q) / (2 * blocks)
    first = np.concatenate([np.cos(angle_qa), -np.sin(angle_qa)], axis=0)
    last = np.concatenate([np.cos(angle_qa.T), -np.sin(angle_qa.T)], axis=1) * (2.0 / full)
    angle_ap = 2.0 * math.pi * np.outer(a, p) / full
    twist = np.stack([np.cos(angle_ap), np.sin(angle_ap)])
    angle_pb = 2.0 * math.pi * (np.outer(p, p) % width) / width
    cos, sin = np.cos(angle_pb), np.sin(angle_pb)
    middle = np.block([[cos, -sin], [sin, cos]])
    half = np.zeros((2 * 2 * width + 2 * blocks + blocks, 2 * width), np.float32)
    half[: 2 * width] = middle
    half[2 * width : 4 * width] = middle.T
    half[4 * width : 4 * width + 2 * blocks, :blocks] = first
    half[4 * width + 2 * blocks :, : 2 * blocks] = last
    wide = np.zeros((8 * blocks, width), np.float32)
    wide[: 2 * blocks] = twist.reshape(2 * blocks, width)
    return jnp.asarray(half.astype(ml_dtypes.bfloat16)), jnp.asarray(wide)


def far_first(step, count):
    up = (step + 1) // 2
    return lax.rem(count // 2 + jnp.where(lax.rem(step, 2) == 1, up, count - step // 2), count)


def far_offsets(count):
    return [(count // 2 + ((i + 1) // 2 if i % 2 else -(i // 2))) % count for i in range(count)]


def main_kernel(
    sizes,
    filt_hbm,
    query_hbm,
    key_hbm,
    value_hbm,
    grad_hbm,
    feat_hbm,
    table_hbm,
    twist_hbm,
    conv_out,
    back_out,
    lag_out,
    qf_out,
    kf_out,
    vf_out,
    grad_out,
    after_out,
    taps,
    filt_ref,
    query_ref,
    key_ref,
    value_ref,
    grad_ref,
    feat_ref,
    table_ref,
    twist_ref,
    ext,
    rim_send,
    rim_recv,
    head_send,
    head_recv,
    feat_next,
    picks,
    heads_send,
    heads_recv,
    filt_send,
    filt_mid,
    filt_recv,
    pair_send,
    pair_recv,
    part_recv,
    conv_send,
    conv_recv,
    lag_send,
    lag_recv,
    wide,
    wide_filt,
    turned,
    filt_spec,
    gate_spec,
    grad_spec,
    product,
    load_sems,
    send_sems,
    recv_sems,
    ring_sem,
):
    ctx, chans, fast = sizes
    tokens, width = query_ref.shape
    middle_rows, back_rows = pl.ds(0, 2 * tokens), pl.ds(2 * tokens, 2 * tokens)
    first_rows, last_rows = pl.ds(4 * tokens, 2 * ctx), pl.ds(4 * tokens + 2 * ctx, ctx)
    me = lax.axis_index("context")
    dp = lax.axis_index("dp")
    slow = ctx // fast
    my_slow, my_fast = me // fast, lax.rem(me, fast)
    following, previous = lax.rem(me + 1, ctx), lax.rem(me + ctx - 1, ctx)
    partner = 1 - dp

    barrier = pltpu.get_barrier_semaphore()

    def tell(sem, device):
        pl.semaphore_signal(sem, inc=1, device_id=device, device_id_type=MESH)

    def in_slow_ring(step):
        return lax.rem(my_slow + far_first(step, slow), slow) * fast + my_fast

    def in_fast_ring(step):
        return my_slow * fast + lax.rem(my_fast + far_first(step, fast), fast)

    @pl.loop(0, slow - 1)
    def _(step):
        tell(barrier, {"context": in_slow_ring(step)})

    @pl.loop(0, fast - 1)
    def _(step):
        tell(barrier, {"context": in_fast_ring(step)})

    tell(barrier, {"context": following})
    tell(barrier, {"context": previous})
    tell(barrier, {"dp": partner})

    loads = [
        pltpu.make_async_copy(src, dst, load_sems.at[i])
        for i, (src, dst) in enumerate(
            (
                (query_hbm, query_ref),
                (key_hbm, key_ref),
                (value_hbm, value_ref),
                (feat_hbm, feat_ref),
                (grad_hbm, grad_ref),
                (filt_hbm, filt_ref),
                (table_hbm, table_ref),
                (twist_hbm.at[pl.ds(0, 2 * ctx)], twist_ref),
            )
        )
    ]
    for load in loads:
        load.start()

    def remote(src, dst, which, device):
        return pltpu.make_async_remote_copy(
            src_ref=src,
            dst_ref=dst,
            send_sem=send_sems.at[which],
            recv_sem=recv_sems.at[which],
            device_id=device,
            device_id_type=MESH,
        )

    fast_places = [lax.rem(my_fast + offset, fast) for offset in far_offsets(fast)]

    def scatter(src, dst, which, with_heads=False):
        def send_row(row, count):
            base = row * fast
            for place in fast_places[:count]:
                peer = base + place
                remote(src.at[peer], dst.at[me], which, {"context": peer}).start()
                if with_heads:
                    remote(heads_send.at[peer], heads_recv.at[me], 8, {"context": peer}).start()

        @pl.loop(0, slow - 1)
        def _(step):
            send_row(lax.rem(my_slow + far_first(step, slow), slow), fast)

        send_row(my_slow, fast - 1)
        dst[me] = src[me]
        if with_heads:
            heads_recv[me] = heads_send[me]

    def ring_scatter(src, dst, place, mine, count, which):
        @pl.loop(0, count - 1)
        def _(step):
            at = lax.rem(mine + far_first(step, count), count)
            remote(src.at[:, at], dst.at[mine], which, {"context": place(step)}).start()

        dst[mine] = src[:, mine]

    def wait_scatter(ref, sems, which):
        rows = ref.at[pl.ds(0, ref.shape[0] - 1)]
        pltpu.make_async_copy(rows, rows, sems.at[which]).wait()

    for load in loads[:3]:
        load.wait()
    for row, rows_ref in enumerate((query_ref, key_ref, value_ref)):
        rim_send[0, 2 * row : 2 * row + 2] = rows_ref[tokens - 16 :].astype(F32)[14:]
    rim_send[0, 6:8] = jnp.zeros((2, width), F32)

    for load in loads[3:]:
        load.wait()
    taps[...] = feat_ref[...].astype(F32)
    for row, rows_ref in enumerate((grad_ref, key_ref, value_ref)):
        head_send[0, 2 * row : 2 * row + 2] = rows_ref[:16].astype(F32)[:2]
    head_send[0, 6:8] = jnp.zeros((2, width), F32)
    by_channel = filt_ref[...].astype(F32).T.reshape(slow, fast, chans, tokens)
    filt_send[...] = by_channel.astype(BF16)

    from_lane = lax.broadcasted_iota(jnp.int32, (tokens, width), 0)
    to_chan = lax.broadcasted_iota(jnp.int32, (tokens, width), 1) % chans
    for kind in range(2):
        for position in range(2):
            pick = from_lane == 2 * (to_chan + chans * kind) + position
            picks[2 * kind + position] = jnp.where(pick, 1.0, 0.0).astype(BF16)

    pl.semaphore_wait(barrier, slow + fast + 1)

    rim_copy = remote(rim_send, rim_recv, 0, {"context": following})
    rim_copy.start()
    head_copy = remote(head_send, head_recv, 6, {"context": previous})
    head_copy.start()

    @pl.loop(0, slow - 1)
    def _(step):
        tell(ring_sem, {"context": in_slow_ring(step)})

    ring_scatter(filt_send, filt_mid, in_fast_ring, my_fast, fast, 1)
    rim_copy.wait()

    keep = jnp.where(me == 0, 0.0, 1.0).astype(F32)

    def featured(rows_ref, which, start=8, count=None):
        if count is None:
            count = tokens
            ext[which, 8 : 8 + tokens] = rows_ref[...].astype(F32)
            ext[which, 6:8] = rim_recv[0, 2 * which : 2 * which + 2] * keep
        total = None
        for lag in range(3):
            tap = taps[which, lag : lag + 1, :]
            term = tap * ext[which, start - lag : start - lag + count]
            total = term if total is None else total + term
        return total.astype(BF16)

    def featured_after(which):
        ext[which, 8 + tokens : 10 + tokens] = head_recv[0, 2 * which : 2 * which + 2]
        return featured(None, which, 8 + tokens, 2).astype(F32)

    query_feat = featured(query_ref, 0)
    qf_out[...] = query_feat
    key_feat = featured(key_ref, 1)
    kf_out[...] = key_feat
    value_feat = featured(value_ref, 2)
    vf_out[...] = value_feat
    grad_out[...] = grad_ref[...]
    gated = (key_feat.astype(F32) * value_feat.astype(F32)).T.reshape(ctx, chans, tokens)
    signal = (grad_ref[...].astype(F32) * query_feat.astype(F32)).T.reshape(ctx, chans, tokens)
    pair_send[...] = jnp.concatenate([gated, signal], axis=1).astype(BF16)
    pl.semaphore_wait(ring_sem, slow - 1)
    scatter(pair_send, pair_recv, 2)
    wait_scatter(filt_mid, recv_sems, 1)
    ring_scatter(filt_mid, filt_recv, in_slow_ring, my_slow, slow, 7)
    head_copy.wait()
    feat_next[0:2] = featured_after(1)
    feat_next[2:4] = featured_after(2)

    def spectra(wide_ref, rows, start, dest):
        for channel in range(chans):
            grid = wide_ref[pl.ds(start + channel, ctx, stride=rows), :].astype(BF16)
            section = jnp.dot(table_ref[first_rows, 0:ctx], grid, preferred_element_type=F32)
            real, imag = section[:ctx], section[ctx:]
            cos, sin = twist_ref[0:ctx], twist_ref[ctx : 2 * ctx]
            here = pl.ds(channel * ctx, ctx)
            turned[here, 0:tokens] = (real * cos + imag * sin).astype(BF16)
            turned[here, tokens : 2 * tokens] = (imag * cos - real * sin).astype(BF16)
        dest[...] = jnp.dot(turned[...], table_ref[middle_rows], preferred_element_type=F32)

    wait_scatter(pair_recv, recv_sems, 2)
    wide[...] = pair_recv[...].astype(F32).reshape(ctx * 2 * chans, tokens)
    spectra(wide, 2 * chans, 0, gate_spec)
    spectra(wide, 2 * chans, chans, grad_spec)

    def parts(ref):
        return ref[:, 0:tokens], ref[:, tokens : 2 * tokens]

    lane = lax.broadcasted_iota(jnp.int32, (ctx, tokens), 1)

    def inverse(real, imag, wide_ref, rows, start, heads=None):
        product[:, 0:tokens] = real.astype(BF16)
        product[:, tokens : 2 * tokens] = imag.astype(BF16)
        gate = jnp.dot(product[...], table_ref[back_rows], preferred_element_type=F32)
        cos, sin = twist_ref[0:ctx], twist_ref[ctx : 2 * ctx]
        for channel in range(chans):
            piece = gate[channel * ctx : (channel + 1) * ctx]
            real, imag = piece[:, :tokens], piece[:, tokens:]
            stacked = jnp.concatenate([real * cos - imag * sin, imag * cos + real * sin], axis=0)
            result = jnp.dot(
                table_ref[last_rows, 0 : 2 * ctx], stacked.astype(BF16), preferred_element_type=F32
            )
            wide_ref[pl.ds(start + channel, ctx, stride=rows), :] = result
            if heads is not None:
                head = jnp.where(lane < 2, result, 0.0)
                heads.append(pltpu.roll(head, 2 * (start + channel), 1))

    gate_real, gate_imag = parts(gate_spec)
    grad_real, grad_imag = parts(grad_spec)
    inverse(
        grad_real * gate_real + grad_imag * gate_imag,
        grad_imag * gate_real - grad_real * gate_imag,
        wide_filt,
        chans,
        0,
    )
    lag_send[...] = wide_filt[...].reshape(ctx, chans, tokens).astype(BF16)
    scatter(lag_send, lag_recv, 5)
    wait_scatter(filt_recv, recv_sems, 7)
    heads = []
    wide_filt[...] = filt_recv[...].astype(F32).reshape(ctx * chans, tokens)
    spectra(wide_filt, chans, 0, filt_spec)
    filt_real, filt_imag = parts(filt_spec)
    gate_real, gate_imag = parts(gate_spec)
    inverse(
        gate_real * filt_real - gate_imag * filt_imag,
        gate_real * filt_imag + gate_imag * filt_real,
        wide,
        2 * chans,
        0,
        heads,
    )
    filt_real, filt_imag = parts(filt_spec)
    grad_real, grad_imag = parts(grad_spec)
    inverse(
        grad_real * filt_real + grad_imag * filt_imag,
        grad_imag * filt_real - grad_real * filt_imag,
        wide,
        2 * chans,
        chans,
        heads,
    )
    heads_send[...] = pltpu.roll(sum(heads), ctx - 1, 0).reshape(ctx, 1, tokens)
    conv_send[...] = wide[...].reshape(ctx, 2 * chans, tokens).astype(BF16)
    scatter(conv_send, conv_recv, 4, True)
    wait_scatter(lag_recv, recv_sems, 5)
    part_copy = remote(lag_recv, part_recv, 3, {"dp": partner})
    part_copy.start()

    wait_scatter(conv_recv, recv_sems, 4)
    both = conv_recv[...].astype(F32)
    conv = both[:, :chans].reshape(width, tokens).T
    back = both[:, chans:].reshape(width, tokens).T
    conv_out[...] = conv.astype(BF16)
    back_out[...] = back.astype(BF16)

    def rounded(x):
        return x.astype(BF16).astype(F32)

    wait_scatter(heads_recv, recv_sems, 8)
    packed = heads_recv[...].reshape(ctx, tokens).astype(BF16)
    holder = lax.broadcasted_iota(jnp.int32, (ctx, width), 0)
    is_mine = lax.broadcasted_iota(jnp.int32, (ctx, width), 1) // chans == holder

    def next_row(kind, position):
        spread = jnp.dot(packed, picks[2 * kind + position], preferred_element_type=F32)
        return jnp.sum(jnp.where(is_mine, spread, 0.0), axis=0, keepdims=True)

    last_keep = jnp.where(me == ctx - 1, 0.0, 1.0).astype(F32)
    for position in range(2):
        conv_next, back_next = next_row(0, position), next_row(1, position)
        at = slice(position, position + 1)
        after_out[at] = rounded(head_recv[0, at] * conv_next) * last_keep
        at = slice(2 + position, 3 + position)
        after_out[at] = rounded(feat_next[at] * back_next) * last_keep
        into = slice(4 + position, 5 + position)
        after_out[into] = rounded(feat_next[slice(position, position + 1)] * back_next) * last_keep
    after_out[6:8] = jnp.zeros((2, width), F32)
    part_copy.wait()
    lag_sum = lag_recv[...].astype(F32) + part_recv[...].astype(F32)
    lag_out[...] = lag_sum.reshape(width, tokens).T.astype(BF16)
    wait_scatter(heads_send, send_sems, 8)
    wait_scatter(filt_mid, send_sems, 1)
    wait_scatter(filt_recv, send_sems, 7)
    wait_scatter(pair_send, send_sems, 2)
    wait_scatter(conv_send, send_sems, 4)
    wait_scatter(lag_send, send_sems, 5)


def final_kernel(
    conv_ref,
    back_ref,
    lag_ref,
    grad_ref,
    qf_ref,
    kf_ref,
    vf_ref,
    after_ref,
    taps_ref,
    out_ref,
    gq_ref,
    gk_ref,
    gv_ref,
    lag_out,
    ext,
):
    tokens = conv_ref.shape[0]
    conv = conv_ref[...].astype(F32)
    back = back_ref[...].astype(F32)
    out_ref[0] = (qf_ref[...].astype(F32) * conv).astype(BF16)

    def unfeatured(rows, which, dest):
        ext[0:tokens] = rows.astype(BF16).astype(F32)
        ext[tokens : tokens + 2] = after_ref[2 * which : 2 * which + 2]
        total = None
        for lag in range(3):
            term = taps_ref[which, lag : lag + 1, :] * ext[lag : lag + tokens]
            total = term if total is None else total + term
        dest[0] = total.astype(BF16)

    unfeatured(grad_ref[...].astype(F32) * conv, 0, gq_ref)
    unfeatured(back * vf_ref[...].astype(F32), 1, gk_ref)
    unfeatured(back * kf_ref[...].astype(F32), 2, gv_ref)
    lag_out[...] = lag_ref[...]


def on_device(ctx, queries, key_gates, values, out_grad, featurizer, long_filter):
    tokens, width = long_filter.shape
    chans = width // ctx
    fast = 1 << ((ctx.bit_length() - 1) // 2)
    table, twist = tables(ctx, tokens)
    slow = ctx // fast
    operands = (
        long_filter,
        queries[0],
        key_gates[0],
        values[0],
        out_grad[0],
        featurizer,
        table,
        twist,
    )
    vmem = pl.BlockSpec(memory_space=pltpu.VMEM)
    like = lambda *shape, dtype=BF16: jax.ShapeDtypeStruct(shape, dtype)
    buf = lambda *shape, dtype=BF16: pltpu.VMEM(shape, dtype)
    results = pl.pallas_call(
        functools.partial(main_kernel, (ctx, chans, fast)),
        out_shape=(
            like(tokens, width),
            like(tokens, width),
            like(tokens, width),
            like(tokens, width),
            like(tokens, width),
            like(tokens, width),
            like(tokens, width),
            like(8, width, dtype=F32),
            like(*featurizer.shape, dtype=F32),
        ),
        in_specs=[pl.BlockSpec(memory_space=pltpu.HBM)] * len(operands),
        out_specs=(vmem,) * 9,
        scratch_shapes=[
            *(buf(*x.shape, dtype=x.dtype) for x in operands[:-1]),
            buf(2 * ctx, tokens, dtype=F32),
            buf(3, tokens + 16, width, dtype=F32),
            buf(1, 8, width, dtype=F32),
            buf(1, 8, width, dtype=F32),
            buf(1, 8, width, dtype=F32),
            buf(1, 8, width, dtype=F32),
            buf(8, width, dtype=F32),
            buf(4, tokens, width),
            buf(ctx, 1, tokens, dtype=F32),
            buf(ctx, 1, tokens, dtype=F32),
            buf(slow, fast, chans, tokens),
            buf(fast, slow, chans, tokens),
            buf(slow, fast, chans, tokens),
            buf(ctx, 2 * chans, tokens),
            buf(ctx, 2 * chans, tokens),
            buf(ctx, chans, tokens),
            buf(ctx, 2 * chans, tokens),
            buf(ctx, 2 * chans, tokens),
            buf(ctx, chans, tokens),
            buf(ctx, chans, tokens),
            buf(ctx * 2 * chans, tokens, dtype=F32),
            buf(ctx * chans, tokens, dtype=F32),
            buf(ctx * chans, 2 * tokens),
            buf(ctx * chans, 2 * tokens, dtype=F32),
            buf(ctx * chans, 2 * tokens, dtype=F32),
            buf(ctx * chans, 2 * tokens, dtype=F32),
            buf(ctx * chans, 2 * tokens),
            pltpu.SemaphoreType.DMA((len(operands),)),
            pltpu.SemaphoreType.DMA((9,)),
            pltpu.SemaphoreType.DMA((9,)),
            pltpu.SemaphoreType.REGULAR,
        ],
        compiler_params=pltpu.CompilerParams(
            collective_id=0, has_side_effects=True, vmem_limit_bytes=GRANT
        ),
        name="exchange",
    )(*(pltpu.with_memory_space_constraint(x, pltpu.HBM) for x in operands))
    conv, back, lag, qf, kf, vf, grad, after, taps = results
    return pl.pallas_call(
        final_kernel,
        out_shape=(like(1, tokens, width),) * 4 + (like(tokens, width),),
        in_specs=[vmem] * 9,
        out_specs=(vmem,) * 5,
        scratch_shapes=[buf(tokens + 16, width, dtype=F32)],
        compiler_params=pltpu.CompilerParams(vmem_limit_bytes=32 * 1024 * 1024),
        name="finish",
    )(conv, back, lag, grad, qf, kf, vf, after, taps)


def solution(mesh):
    in_specs = (
        P("dp", "context", "tensor"),
        P("dp", "context", "tensor"),
        P("dp", "context", "tensor"),
        P("dp", "context", "tensor"),
        P(None, None, "tensor"),
        P("context", "tensor"),
    )
    out_specs = (
        P("dp", "context", "tensor"),
        P("dp", "context", "tensor"),
        P("dp", "context", "tensor"),
        P("dp", "context", "tensor"),
        P("context", "tensor"),
    )
    return jax.shard_map(
        functools.partial(on_device, mesh.shape["context"]),
        mesh=mesh,
        in_specs=in_specs,
        out_specs=out_specs,
        check_vma=False,
    )
```

```python
import functools
import math

import ml_dtypes
import numpy as np

import jax
import jax.numpy as jnp
from jax import lax
from jax.experimental import pallas as pl
from jax.experimental.pallas import tpu as pltpu
from jax.sharding import PartitionSpec as P

MESH = pl.DeviceIdType.MESH
F32 = jnp.float32
BF16 = jnp.bfloat16
GRANT = 40000 * 1024


def tables(blocks, width):
    full = 2 * blocks * width
    a = np.arange(blocks) + 0.5
    q = np.arange(blocks)
    p = np.arange(width)
    angle_qa = 2.0 * math.pi * np.outer(a, q) / (2 * blocks)
    first = np.concatenate([np.cos(angle_qa), -np.sin(angle_qa)], axis=0)
    last = np.concatenate([np.cos(angle_qa.T), -np.sin(angle_qa.T)], axis=1) * (2.0 / full)
    angle_ap = 2.0 * math.pi * np.outer(a, p) / full
    twist = np.stack([np.cos(angle_ap), np.sin(angle_ap)])
    angle_pb = 2.0 * math.pi * (np.outer(p, p) % width) / width
    cos, sin = np.cos(angle_pb), np.sin(angle_pb)
    middle = np.block([[cos, -sin], [sin, cos]])
    half = np.zeros((2 * 2 * width + 2 * blocks + blocks, 2 * width), np.float32)
    half[: 2 * width] = middle
    half[2 * width : 4 * width] = middle.T
    half[4 * width : 4 * width + 2 * blocks, :blocks] = first
    half[4 * width + 2 * blocks :, : 2 * blocks] = last
    wide = np.zeros((8 * blocks, width), np.float32)
    wide[: 2 * blocks] = twist.reshape(2 * blocks, width)
    return jnp.asarray(half.astype(ml_dtypes.bfloat16)), jnp.asarray(wide)


def far_first(step, count):
    up = (step + 1) // 2
    return lax.rem(count // 2 + jnp.where(lax.rem(step, 2) == 1, up, count - step // 2), count)


def far_offsets(count):
    return [(count // 2 + ((i + 1) // 2 if i % 2 else -(i // 2))) % count for i in range(count)]


def main_kernel(
    sizes,
    filt_hbm,
    query_hbm,
    key_hbm,
    value_hbm,
    grad_hbm,
    feat_hbm,
    table_hbm,
    twist_hbm,
    conv_out,
    back_out,
    lag_out,
    qf_out,
    kf_out,
    vf_out,
    grad_out,
    after_out,
    taps,
    filt_ref,
    query_ref,
    key_ref,
    value_ref,
    grad_ref,
    feat_ref,
    table_ref,
    twist_ref,
    ext,
    rim_send,
    rim_recv,
    head_send,
    head_recv,
    feat_next,
    picks,
    heads_send,
    heads_recv,
    filt_send,
    filt_mid,
    filt_recv,
    pair_send,
    pair_recv,
    part_recv,
    conv_send,
    conv_recv,
    lag_send,
    lag_recv,
    wide,
    wide_filt,
    turned,
    filt_spec,
    gate_spec,
    grad_spec,
    product,
    load_sems,
    send_sems,
    recv_sems,
    ring_sem,
):
    ctx, chans, fast = sizes
    tokens, width = query_ref.shape
    middle_rows, back_rows = pl.ds(0, 2 * tokens), pl.ds(2 * tokens, 2 * tokens)
    first_rows, last_rows = pl.ds(4 * tokens, 2 * ctx), pl.ds(4 * tokens + 2 * ctx, ctx)
    me = lax.axis_index("context")
    dp = lax.axis_index("dp")
    slow = ctx // fast
    my_slow, my_fast = me // fast, lax.rem(me, fast)
    following, previous = lax.rem(me + 1, ctx), lax.rem(me + ctx - 1, ctx)
    partner = 1 - dp

    barrier = pltpu.get_barrier_semaphore()

    def tell(sem, device):
        pl.semaphore_signal(sem, inc=1, device_id=device, device_id_type=MESH)

    def in_slow_ring(step):
        return lax.rem(my_slow + far_first(step, slow), slow) * fast + my_fast

    def in_fast_ring(step):
        return my_slow * fast + lax.rem(my_fast + far_first(step, fast), fast)

    @pl.loop(0, slow - 1)
    def _(step):
        tell(barrier, {"context": in_slow_ring(step)})

    @pl.loop(0, fast - 1)
    def _(step):
        tell(barrier, {"context": in_fast_ring(step)})

    tell(barrier, {"context": following})
    tell(barrier, {"context": previous})
    tell(barrier, {"dp": partner})

    loads = [
        pltpu.make_async_copy(src, dst, load_sems.at[i])
        for i, (src, dst) in enumerate(
            (
                (query_hbm, query_ref),
                (key_hbm, key_ref),
                (value_hbm, value_ref),
                (feat_hbm, feat_ref),
                (grad_hbm, grad_ref),
                (filt_hbm, filt_ref),
                (table_hbm, table_ref),
                (twist_hbm.at[pl.ds(0, 2 * ctx)], twist_ref),
            )
        )
    ]
    for load in loads:
        load.start()

    def remote(src, dst, which, device):
        return pltpu.make_async_remote_copy(
            src_ref=src,
            dst_ref=dst,
            send_sem=send_sems.at[which],
            recv_sem=recv_sems.at[which],
            device_id=device,
            device_id_type=MESH,
        )

    fast_places = [lax.rem(my_fast + offset, fast) for offset in far_offsets(fast)]

    def scatter(src, dst, which):
        def send_row(row, count):
            base = row * fast
            for place in fast_places[:count]:
                peer = base + place
                remote(src.at[peer], dst.at[me], which, {"context": peer}).start()

        @pl.loop(0, slow - 1)
        def _(step):
            send_row(lax.rem(my_slow + far_first(step, slow), slow), fast)

        send_row(my_slow, fast - 1)
        dst[me] = src[me]

    def ring_scatter(src, dst, place, mine, count, which):
        @pl.loop(0, count - 1)
        def _(step):
            at = lax.rem(mine + far_first(step, count), count)
            remote(src.at[:, at], dst.at[mine], which, {"context": place(step)}).start()

        dst[mine] = src[:, mine]

    def wait_scatter(ref, sems, which):
        rows = ref.at[pl.ds(0, ref.shape[0] - 1)]
        pltpu.make_async_copy(rows, rows, sems.at[which]).wait()

    for load in loads[:3]:
        load.wait()
    for row, rows_ref in enumerate((query_ref, key_ref, value_ref)):
        rim_send[0, 2 * row : 2 * row + 2] = rows_ref[tokens - 16 :].astype(F32)[14:]
    rim_send[0, 6:8] = jnp.zeros((2, width), F32)

    for load in loads[3:]:
        load.wait()
    taps[...] = feat_ref[...].astype(F32)
    for row, rows_ref in enumerate((grad_ref, key_ref, value_ref)):
        head_send[0, 2 * row : 2 * row + 2] = rows_ref[:16].astype(F32)[:2]
    head_send[0, 6:8] = jnp.zeros((2, width), F32)
    by_channel = filt_ref[...].astype(F32).T.reshape(slow, fast, chans, tokens)
    filt_send[...] = by_channel.astype(BF16)

    from_lane = lax.broadcasted_iota(jnp.int32, (tokens, width), 0)
    to_chan = lax.broadcasted_iota(jnp.int32, (tokens, width), 1) % chans
    for kind in range(2):
        for position in range(2):
            pick = from_lane == 2 * (to_chan + chans * kind) + position
            picks[2 * kind + position] = jnp.where(pick, 1.0, 0.0).astype(BF16)

    pl.semaphore_wait(barrier, slow + fast + 1)

    rim_copy = remote(rim_send, rim_recv, 0, {"context": following})
    rim_copy.start()
    head_copy = remote(head_send, head_recv, 6, {"context": previous})
    head_copy.start()

    @pl.loop(0, slow - 1)
    def _(step):
        tell(ring_sem, {"context": in_slow_ring(step)})

    ring_scatter(filt_send, filt_mid, in_fast_ring, my_fast, fast, 1)
    rim_copy.wait()

    keep = jnp.where(me == 0, 0.0, 1.0).astype(F32)

    def featured(rows_ref, which, start=8, count=None):
        if count is None:
            count = tokens
            ext[which, 8 : 8 + tokens] = rows_ref[...].astype(F32)
            ext[which, 6:8] = rim_recv[0, 2 * which : 2 * which + 2] * keep
        total = None
        for lag in range(3):
            tap = taps[which, lag : lag + 1, :]
            term = tap * ext[which, start - lag : start - lag + count]
            total = term if total is None else total + term
        return total.astype(BF16)

    def featured_after(which):
        ext[which, 8 + tokens : 10 + tokens] = head_recv[0, 2 * which : 2 * which + 2]
        return featured(None, which, 8 + tokens, 2).astype(F32)

    query_feat = featured(query_ref, 0)
    qf_out[...] = query_feat
    key_feat = featured(key_ref, 1)
    kf_out[...] = key_feat
    value_feat = featured(value_ref, 2)
    vf_out[...] = value_feat
    grad_out[...] = grad_ref[...]
    gated = (key_feat.astype(F32) * value_feat.astype(F32)).T.reshape(ctx, chans, tokens)
    signal = (grad_ref[...].astype(F32) * query_feat.astype(F32)).T.reshape(ctx, chans, tokens)
    pair_send[...] = jnp.concatenate([gated, signal], axis=1).astype(BF16)
    pl.semaphore_wait(ring_sem, slow - 1)
    scatter(pair_send, pair_recv, 2)
    wait_scatter(filt_mid, recv_sems, 1)
    ring_scatter(filt_mid, filt_recv, in_slow_ring, my_slow, slow, 7)
    head_copy.wait()
    feat_next[0:2] = featured_after(1)
    feat_next[2:4] = featured_after(2)

    def spectra(wide_ref, rows, start, dest):
        for channel in range(chans):
            grid = wide_ref[pl.ds(start + channel, ctx, stride=rows), :].astype(BF16)
            section = jnp.dot(table_ref[first_rows, 0:ctx], grid, preferred_element_type=F32)
            real, imag = section[:ctx], section[ctx:]
            cos, sin = twist_ref[0:ctx], twist_ref[ctx : 2 * ctx]
            here = pl.ds(channel * ctx, ctx)
            turned[here, 0:tokens] = (real * cos + imag * sin).astype(BF16)
            turned[here, tokens : 2 * tokens] = (imag * cos - real * sin).astype(BF16)
        dest[...] = jnp.dot(turned[...], table_ref[middle_rows], preferred_element_type=F32)

    wait_scatter(pair_recv, recv_sems, 2)
    wide[...] = pair_recv[...].astype(F32).reshape(ctx * 2 * chans, tokens)
    spectra(wide, 2 * chans, 0, gate_spec)
    spectra(wide, 2 * chans, chans, grad_spec)

    def parts(ref):
        return ref[:, 0:tokens], ref[:, tokens : 2 * tokens]

    lane = lax.broadcasted_iota(jnp.int32, (ctx, tokens), 1)

    def inverse(real, imag, wide_ref, rows, start, heads=None):
        product[:, 0:tokens] = real.astype(BF16)
        product[:, tokens : 2 * tokens] = imag.astype(BF16)
        gate = jnp.dot(product[...], table_ref[back_rows], preferred_element_type=F32)
        cos, sin = twist_ref[0:ctx], twist_ref[ctx : 2 * ctx]
        for channel in range(chans):
            piece = gate[channel * ctx : (channel + 1) * ctx]
            real, imag = piece[:, :tokens], piece[:, tokens:]
            stacked = jnp.concatenate([real * cos - imag * sin, imag * cos + real * sin], axis=0)
            result = jnp.dot(
                table_ref[last_rows, 0 : 2 * ctx], stacked.astype(BF16), preferred_element_type=F32
            )
            wide_ref[pl.ds(start + channel, ctx, stride=rows), :] = result
            if heads is not None:
                head = jnp.where(lane < 2, result, 0.0)
                heads.append(pltpu.roll(head, 2 * (start + channel), 1))

    gate_real, gate_imag = parts(gate_spec)
    grad_real, grad_imag = parts(grad_spec)
    inverse(
        grad_real * gate_real + grad_imag * gate_imag,
        grad_imag * gate_real - grad_real * gate_imag,
        wide_filt,
        chans,
        0,
    )
    lag_send[...] = wide_filt[...].reshape(ctx, chans, tokens).astype(BF16)
    scatter(lag_send, lag_recv, 5)
    wait_scatter(filt_recv, recv_sems, 7)
    heads = []
    wide_filt[...] = filt_recv[...].astype(F32).reshape(ctx * chans, tokens)
    spectra(wide_filt, chans, 0, filt_spec)
    filt_real, filt_imag = parts(filt_spec)
    gate_real, gate_imag = parts(gate_spec)
    inverse(
        gate_real * filt_real - gate_imag * filt_imag,
        gate_real * filt_imag + gate_imag * filt_real,
        wide,
        2 * chans,
        0,
        heads,
    )
    filt_real, filt_imag = parts(filt_spec)
    grad_real, grad_imag = parts(grad_spec)
    inverse(
        grad_real * filt_real + grad_imag * filt_imag,
        grad_imag * filt_real - grad_real * filt_imag,
        wide,
        2 * chans,
        chans,
        heads,
    )
    heads_send[...] = pltpu.roll(sum(heads), ctx - 1, 0).reshape(ctx, 1, tokens)
    conv_send[...] = wide[...].reshape(ctx, 2 * chans, tokens).astype(BF16)
    scatter(conv_send, conv_recv, 4)
    scatter(heads_send, heads_recv, 8)
    wait_scatter(lag_recv, recv_sems, 5)
    part_copy = remote(lag_recv, part_recv, 3, {"dp": partner})
    part_copy.start()

    wait_scatter(conv_recv, recv_sems, 4)
    both = conv_recv[...].astype(F32)
    conv = both[:, :chans].reshape(width, tokens).T
    back = both[:, chans:].reshape(width, tokens).T
    conv_out[...] = conv.astype(BF16)
    back_out[...] = back.astype(BF16)

    def rounded(x):
        return x.astype(BF16).astype(F32)

    wait_scatter(heads_recv, recv_sems, 8)
    packed = heads_recv[...].reshape(ctx, tokens).astype(BF16)
    holder = lax.broadcasted_iota(jnp.int32, (ctx, width), 0)
    is_mine = lax.broadcasted_iota(jnp.int32, (ctx, width), 1) // chans == holder

    def next_row(kind, position):
        spread = jnp.dot(packed, picks[2 * kind + position], preferred_element_type=F32)
        return jnp.sum(jnp.where(is_mine, spread, 0.0), axis=0, keepdims=True)

    last_keep = jnp.where(me == ctx - 1, 0.0, 1.0).astype(F32)
    for position in range(2):
        conv_next, back_next = next_row(0, position), next_row(1, position)
        at = slice(position, position + 1)
        after_out[at] = rounded(head_recv[0, at] * conv_next) * last_keep
        at = slice(2 + position, 3 + position)
        after_out[at] = rounded(feat_next[at] * back_next) * last_keep
        into = slice(4 + position, 5 + position)
        after_out[into] = rounded(feat_next[slice(position, position + 1)] * back_next) * last_keep
    after_out[6:8] = jnp.zeros((2, width), F32)
    part_copy.wait()
    lag_sum = lag_recv[...].astype(F32) + part_recv[...].astype(F32)
    lag_out[...] = lag_sum.reshape(width, tokens).T.astype(BF16)
    wait_scatter(heads_send, send_sems, 8)
    wait_scatter(filt_mid, send_sems, 1)
    wait_scatter(filt_recv, send_sems, 7)
    wait_scatter(pair_send, send_sems, 2)
    wait_scatter(conv_send, send_sems, 4)
    wait_scatter(lag_send, send_sems, 5)


def final_kernel(
    conv_ref,
    back_ref,
    lag_ref,
    grad_ref,
    qf_ref,
    kf_ref,
    vf_ref,
    after_ref,
    taps_ref,
    out_ref,
    gq_ref,
    gk_ref,
    gv_ref,
    lag_out,
    ext,
):
    tokens = conv_ref.shape[0]
    conv = conv_ref[...].astype(F32)
    back = back_ref[...].astype(F32)
    out_ref[0] = (qf_ref[...].astype(F32) * conv).astype(BF16)

    def unfeatured(rows, which, dest):
        ext[0:tokens] = rows.astype(BF16).astype(F32)
        ext[tokens : tokens + 2] = after_ref[2 * which : 2 * which + 2]
        total = None
        for lag in range(3):
            term = taps_ref[which, lag : lag + 1, :] * ext[lag : lag + tokens]
            total = term if total is None else total + term
        dest[0] = total.astype(BF16)

    unfeatured(grad_ref[...].astype(F32) * conv, 0, gq_ref)
    unfeatured(back * vf_ref[...].astype(F32), 1, gk_ref)
    unfeatured(back * kf_ref[...].astype(F32), 2, gv_ref)
    lag_out[...] = lag_ref[...]


def on_device(ctx, queries, key_gates, values, out_grad, featurizer, long_filter):
    tokens, width = long_filter.shape
    chans = width // ctx
    fast = 1 << ((ctx.bit_length() - 1) // 2)
    table, twist = tables(ctx, tokens)
    slow = ctx // fast
    operands = (
        long_filter,
        queries[0],
        key_gates[0],
        values[0],
        out_grad[0],
        featurizer,
        table,
        twist,
    )
    vmem = pl.BlockSpec(memory_space=pltpu.VMEM)
    like = lambda *shape, dtype=BF16: jax.ShapeDtypeStruct(shape, dtype)
    buf = lambda *shape, dtype=BF16: pltpu.VMEM(shape, dtype)
    results = pl.pallas_call(
        functools.partial(main_kernel, (ctx, chans, fast)),
        out_shape=(
            like(tokens, width),
            like(tokens, width),
            like(tokens, width),
            like(tokens, width),
            like(tokens, width),
            like(tokens, width),
            like(tokens, width),
            like(8, width, dtype=F32),
            like(*featurizer.shape, dtype=F32),
        ),
        in_specs=[pl.BlockSpec(memory_space=pltpu.HBM)] * len(operands),
        out_specs=(vmem,) * 9,
        scratch_shapes=[
            *(buf(*x.shape, dtype=x.dtype) for x in operands[:-1]),
            buf(2 * ctx, tokens, dtype=F32),
            buf(3, tokens + 16, width, dtype=F32),
            buf(1, 8, width, dtype=F32),
            buf(1, 8, width, dtype=F32),
            buf(1, 8, width, dtype=F32),
            buf(1, 8, width, dtype=F32),
            buf(8, width, dtype=F32),
            buf(4, tokens, width),
            buf(ctx, 1, tokens, dtype=F32),
            buf(ctx, 1, tokens, dtype=F32),
            buf(slow, fast, chans, tokens),
            buf(fast, slow, chans, tokens),
            buf(slow, fast, chans, tokens),
            buf(ctx, 2 * chans, tokens),
            buf(ctx, 2 * chans, tokens),
            buf(ctx, chans, tokens),
            buf(ctx, 2 * chans, tokens),
            buf(ctx, 2 * chans, tokens),
            buf(ctx, chans, tokens),
            buf(ctx, chans, tokens),
            buf(ctx * 2 * chans, tokens, dtype=F32),
            buf(ctx * chans, tokens, dtype=F32),
            buf(ctx * chans, 2 * tokens),
            buf(ctx * chans, 2 * tokens, dtype=F32),
            buf(ctx * chans, 2 * tokens, dtype=F32),
            buf(ctx * chans, 2 * tokens, dtype=F32),
            buf(ctx * chans, 2 * tokens),
            pltpu.SemaphoreType.DMA((len(operands),)),
            pltpu.SemaphoreType.DMA((9,)),
            pltpu.SemaphoreType.DMA((9,)),
            pltpu.SemaphoreType.REGULAR,
        ],
        compiler_params=pltpu.CompilerParams(
            collective_id=0, has_side_effects=True, vmem_limit_bytes=GRANT
        ),
        name="exchange",
    )(*(pltpu.with_memory_space_constraint(x, pltpu.HBM) for x in operands))
    conv, back, lag, qf, kf, vf, grad, after, taps = results
    return pl.pallas_call(
        final_kernel,
        out_shape=(like(1, tokens, width),) * 4 + (like(tokens, width),),
        in_specs=[vmem] * 9,
        out_specs=(vmem,) * 5,
        scratch_shapes=[buf(tokens + 16, width, dtype=F32)],
        compiler_params=pltpu.CompilerParams(vmem_limit_bytes=32 * 1024 * 1024),
        name="finish",
    )(conv, back, lag, grad, qf, kf, vf, after, taps)


def solution(mesh):
    in_specs = (
        P("dp", "context", "tensor"),
        P("dp", "context", "tensor"),
        P("dp", "context", "tensor"),
        P("dp", "context", "tensor"),
        P(None, None, "tensor"),
        P("context", "tensor"),
    )
    out_specs = (
        P("dp", "context", "tensor"),
        P("dp", "context", "tensor"),
        P("dp", "context", "tensor"),
        P("dp", "context", "tensor"),
        P("context", "tensor"),
    )
    return jax.shard_map(
        functools.partial(on_device, mesh.shape["context"]),
        mesh=mesh,
        in_specs=in_specs,
        out_specs=out_specs,
        check_vma=False,
    )
```
